256 devices in a mesh: row: 16 (over x, y), col: 16 (over z, core).
Axes of the slice: x: 4, y: 4, z: 8, core: 2. Of those that a mesh axis runs over, the one named last changes fastest.
Arguments:
- tiles: bfloat16 [64, 32, 128, 128], P('row', 'col'), may hold values from -6 to 6
- pattern: int32 [64, 32], P('row', 'col'), may hold values from -1 to 3, as said below
Outputs:
- sign_tiles: bfloat16 [64, 32, 128, 128], P('row', 'col')
- square_tiles: bfloat16 [64, 32, 128, 128], P('row', 'col')
The draws below stay inside these ranges and needn't reach their ends.
Inputs may be any that keep to these rules, and one draw needn't show every extreme that they name: `pattern`: -1 marks an empty slot; the used block columns of one block row are distinct; the first slot of every panel is used, and every block row stores its diagonal block.
All inputs are finite; a program needn't handle non-finite values.
Results may differ from the reference program's by a relative error of at most 0.0058.
Values may be sent and summed in bfloat16 or wider, within the bound.
A program may use at most 64 MiB of HBM per device.

```python
import jax
import jax.numpy as jnp
from jax import lax

BS = 128
KP = 2
ITERS = 2
NB = 64
PANEL = 4
SLOTS = 32
N_COL = 16


def draw_pattern(key, part):
    key = jax.random.fold_in(key, 11)
    perm_key, keep_key = jax.random.split(key)
    keys = jax.random.split(perm_key, NB * N_COL)
    perms = jax.vmap(lambda k: jax.random.permutation(k, PANEL))(keys).reshape(NB, N_COL, PANEL).astype(jnp.int32)
    rows = jnp.arange(NB, dtype=jnp.int32)
    own = (rows % PANEL)[:, None, None]
    is_diag = (jnp.arange(N_COL, dtype=jnp.int32)[None, :] == (rows // PANEL)[:, None])[:, :, None]
    first = perms[:, :, :1]
    swapped = jnp.where(perms == own, first, perms)
    block_position = jnp.arange(PANEL, dtype=jnp.int32)[None, None, :]
    swapped = jnp.where(block_position == 0, own, swapped)
    chosen = jnp.where(is_diag, swapped, perms)[:, :, :KP]
    keep = jax.random.randint(keep_key, (NB, N_COL, KP), 0, 5) < 3
    slot = jnp.arange(KP, dtype=jnp.int32)[None, None, :]
    keep = keep | (slot == 0)
    forced = (rows[:, None, None] == 0) & (jnp.arange(N_COL, dtype=jnp.int32)[None, :, None] == N_COL - 1) & (slot == KP - 1)
    keep = keep & jnp.logical_not(forced)
    return jnp.where(keep, chosen, -1).reshape(NB, N_COL * KP).astype(jnp.int32)


def block_levels(own_key, extent, cuts, least, largest):
    def one(axis_at, parts):
        draws = jax.random.uniform(jax.random.fold_in(jax.random.fold_in(own_key, 6), axis_at), (parts,), jnp.float32, least / len(cuts), largest / len(cuts))
        return jnp.repeat(jnp.exp(draws), extent[axis_at] // parts).reshape((-1,) + (1,) * (len(extent) - axis_at - 1))

    factor_of = one(*cuts[0])
    for cut in cuts[1:]:
        factor_of = factor_of * one(*cut)
    return factor_of


def bell_draw(own_key, extent, scale, reach, shards=(), kind=jnp.bfloat16):
    values = jax.random.normal(own_key, extent, jnp.float32) * scale
    if len(shards) > 0:
        values = block_levels(own_key, extent, shards, -0.22, 0.18) * values
    return jnp.clip(values, min=-reach, max=reach).astype(kind)


def setup_inputs(seed: int = 0) -> dict:
    key_of = jax.random.split(jax.random.key(seed), 3)
    tiles = bell_draw(key_of[0], (NB, SLOTS, BS, BS), 1.0, 6.0, ((0, 16), (1, 16)))
    pattern = draw_pattern(jax.random.fold_in(key_of[2], 71), 0)
    return {"tiles": tiles, "pattern": pattern}


def columns_of(pattern):
    valid = pattern >= 0
    slot = jnp.arange(SLOTS, dtype=jnp.int32)
    gcol = jnp.where(valid, (slot // KP)[None, :] * PANEL + pattern, -1).astype(jnp.int32)
    return gcol, valid


def restricted(left_operand, right, gcol, valid):
    def one_row(index_entry):
        mine = gcol[index_entry]
        mine_ok = valid[index_entry]
        kidx = jnp.where(mine_ok, mine, 0).astype(jnp.int32)
        right_cols = gcol[kidx]
        right_ok = valid[kidx]
        match = (right_cols[:, :, None] == mine[None, None, :]) & right_ok[:, :, None]
        match = match & mine_ok[:, None, None] & mine_ok[None, None, :]
        picked = jnp.argmax(match, axis=1).astype(jnp.int32)
        found = jnp.any(match, axis=1)
        block_list = right[kidx[:, None], picked]
        block_list = jnp.where(found[:, :, None, None], block_list.astype(jnp.float32), 0.0)
        return jnp.einsum("pro,phoy->hry", left_operand[index_entry].astype(jnp.float32), block_list)
    return lax.map(one_row, jnp.arange(NB, dtype=jnp.int32))


def reference(tiles, pattern):
    gcol, valid = columns_of(pattern)
    keep = valid[:, :, None, None]
    scale = 2.0 * SLOTS * BS
    sign = jnp.where(keep, tiles, jnp.zeros_like(tiles))
    square = sign
    for step in range(ITERS):
        square = (restricted(sign, sign, gcol, valid) / scale).astype(jnp.bfloat16)
        product = restricted(sign, square, gcol, valid)
        sign = jnp.where(keep, 1.5 * sign.astype(jnp.float32) - 0.5 * product, 0.0).astype(jnp.bfloat16)
    return sign, square
```

```python
import functools

import jax
import jax.numpy as jnp
from jax import lax
from jax.experimental import pallas as pl
from jax.experimental.pallas import tpu as pltpu
from jax.sharding import PartitionSpec as P

ITERS = 2
SIDE = 4
RING = 8
LINES = 16
BLOCKS = 8
MESH = pl.DeviceIdType.MESH

PARTS = {"w": (0, 4), "a": (0, 2), "b": (2, 4)}
ROW_KEYS = []
for _h in (0, 1):
    ROW_KEYS += [(_h, -1, 0, "w"), (_h, 1, 0, "w"), (_h, 2, 0, "a"), (_h, 2, 0, "b")]
    for _f in (0, -1, 1, 2):
        ROW_KEYS += [(_h, _f, -1, "w"), (_h, _f, 1, "w"), (_h, _f, 2, "a"), (_h, _f, 2, "b")]
ROW_ID = {key: n for n, key in enumerate(ROW_KEYS)}

UP = [(1, 0, 1), (1, 1, 1), (1, 0, 2), (1, 1, 2), (1, 0, 3), (1, 1, 3), (1, 0, 4)]
DOWN = [(-1, 1, 1), (-1, 0, 1), (-1, 1, 2), (-1, 0, 2), (-1, 1, 3), (-1, 0, 3), (-1, 1, 4)]
COL_KEYS = UP + DOWN + [("c", 0, 0, 0)] + [("c",) + key for key in UP + DOWN]
COL_ID = {key: n for n, key in enumerate(COL_KEYS)}


def kernel(
    tiles, pattern, sign_out, square_out,
    left, right, loc, acc, prow, pcol, srow, scol, table,
    psend, precv, plocal, rsend, rrecv, csend, crecv,
):
    row, col = lax.axis_index("row"), lax.axis_index("col")
    x, y = lax.div(row, SIDE), lax.rem(row, SIDE)
    z, core = lax.div(col, 2), lax.rem(col, 2)

    def row_at(dx, dy):
        return lax.rem(x + dx + SIDE, SIDE) * SIDE + lax.rem(y + dy + SIDE, SIDE)

    def col_at(dz, own_core=True):
        return lax.rem(z + dz + RING, RING) * 2 + (core if own_core else 1 - core)

    def row_copy(half, key, sending):
        h, f, s, part = key
        second = s != 0
        step = {-1: 1, 1: -1}.get(s if second else f) or (1 if part == "a" else -1)
        if sending:
            if second:
                s = s + step if s != 2 else -step
            else:
                f = f + step if f != 2 else -step
        lo, hi = PARTS[part]
        off = (f, s) if h == 0 else (s, f)
        ref = right.at[half, row_at(*off), pl.ds(h * 4 + lo, hi - lo)]
        to_x = (h == 0) != second
        target = row_at(step, 0) if to_x else row_at(0, step)
        n = ROW_ID[key]
        return pltpu.make_async_remote_copy(
            src_ref=ref, dst_ref=ref, send_sem=rsend.at[half, n], recv_sem=rrecv.at[half, n],
            device_id=(target, col), device_id_type=MESH,
        )

    def row_send(half, *keys):
        for key in keys:
            row_copy(half, key, True).start()

    def row_wait(half, *keys):
        for key in keys:
            row_copy(half, key, False).wait_recv()

    def col_copy(it, key, sending):
        if key[0] == "c":
            _, sign, h, d = key
            ref_col = col_at(-sign * d, sending)
            target = col_at(0, False)
            lo, n = (0, 8) if d == 0 else (h * 4, 4)
        else:
            sign, h, d = key
            ref_col = col_at(-sign * (d - 1 if sending else d))
            target = col_at(sign)
            lo, n = h * 4, 4
        ref = left.at[it, ref_col, pl.ds(lo, n)]
        k = COL_ID[key]
        return pltpu.make_async_remote_copy(
            src_ref=ref, dst_ref=ref, send_sem=csend.at[it, k], recv_sem=crecv.at[it, k],
            device_id=(row, target), device_id_type=MESH,
        )

    def col_send(it, *keys):
        for key in keys:
            col_copy(it, key, True).start()

    def col_event(it, n):
        for key in (UP[n], DOWN[n]):
            col_copy(it, key, False).wait_recv()
            sign, h, d = key
            if (sign, h, d + 1) in COL_ID:
                col_send(it, (sign, h, d + 1))
            col_send(it, ("c",) + key)

    def cross_wait(it, least, most):
        for key in COL_KEYS:
            if key[0] == "c" and least <= key[3] <= most:
                col_copy(it, key, False).wait_recv()

    def row_start(half):
        for h in (0, 1):
            row_send(half, (h, -1, 0, "w"), (h, 1, 0, "w"))
        for h in (1, 0):
            row_send(half, (h, 0, -1, "w"), (h, 0, 1, "w"))

    def row_e1(half):
        for h in (0, 1):
            for f, part in ((-1, "a"), (1, "b")):
                row_wait(half, (h, f, 0, "w"))
                row_send(half, (h, 2, 0, part), (h, f, -1, "w"), (h, f, 1, "w"))

    def row_fan(half, f):
        for h in (0, 1):
            for s, part in ((-1, "a"), (1, "b")):
                row_wait(half, (h, f, s, "w"))
                row_send(half, (h, f, 2, part))

    def row_e3(half):
        for h in (0, 1):
            row_wait(half, (h, 2, 0, "a"), (h, 2, 0, "b"))
            row_send(half, (h, 2, -1, "w"), (h, 2, 1, "w"))

    def row_last(half, *fs):
        for f in fs:
            for h in (0, 1):
                row_wait(half, (h, f, 2, "a"), (h, f, 2, "b"))

    def piece(it, half, r):
        loc[0:BLOCKS] = right[half, r]
        for i in range(4):
            at = r * 16 + i * 4
            a = jnp.concatenate([left[it, r, 2 * i], left[it, r, 2 * i + 1]], axis=1)
            b = jnp.concatenate(
                [
                    jnp.concatenate([loc[table[at + 2 * s]], loc[table[at + 2 * s + 1]]], axis=1)
                    for s in (0, 1)
                ],
                axis=0,
            )
            acc[i] += jnp.dot(a, b, preferred_element_type=jnp.float32)

    def make_table(first, count):
        @pl.loop(first, first + count)
        def _(r):
            for i in range(4):
                for s in range(2):
                    k = scol[r, i, s]
                    at_k = jnp.maximum(k, 0)
                    j0, j1 = srow[r, at_k, 0], srow[r, at_k, 1]
                    for t in range(2):
                        j = srow[row, i, t]
                        ok = (k >= 0) & (j >= 0)
                        found = jnp.where(j0 == j, 2 * at_k, jnp.where(j1 == j, 2 * at_k + 1, BLOCKS))
                        table[r * 16 + i * 4 + s * 2 + t] = jnp.where(ok, found, BLOCKS)

    def patterns():
        for land, smem, n in ((prow, srow, 0), (pcol, scol, 1)):
            some = land.at[pl.ds(0, LINES - 1)]
            pltpu.make_async_copy(some, some, precv.at[n]).wait()
            pltpu.make_async_copy(land, smem, plocal.at[n]).start()
        for land, smem, n in ((prow, srow, 0), (pcol, scol, 1)):
            pltpu.make_async_copy(land, smem, plocal.at[n]).wait()

    padded = jnp.full((8, 128), -1, jnp.int32)
    prow[row] = padded
    pcol[col] = padded
    prow[row, 0:4, 0:2] = pattern[...]
    pcol[col, 0:4, 0:2] = pattern[...]
    own = tiles[...].reshape(BLOCKS, 128, 128)
    left[0, col] = own
    right[0, row] = own
    loc[BLOCKS] = jnp.zeros((128, 128), jnp.bfloat16)

    barrier = pltpu.get_barrier_semaphore()

    @pl.loop(1, LINES)
    def _(d):
        pl.semaphore_signal(barrier, inc=1, device_id=(lax.rem(row + d, LINES), col), device_id_type=MESH)
        pl.semaphore_signal(barrier, inc=1, device_id=(row, lax.rem(col + d, LINES)), device_id_type=MESH)

    pl.semaphore_wait(barrier, 2 * (LINES - 1))

    def pattern_copy(d, n):
        land = (prow.at[row], pcol.at[col])[n]
        to = ((lax.rem(row + d, LINES), col), (row, lax.rem(col + d, LINES)))[n]
        return pltpu.make_async_remote_copy(
            src_ref=land, dst_ref=land, send_sem=psend.at[n], recv_sem=precv.at[n],
            device_id=to, device_id_type=MESH,
        )

    @pl.loop(0, ITERS)
    def _(it):
        first, second = 2 * it, 2 * it + 1

        row_start(first)
        col_send(it, UP[0], DOWN[0], UP[1], DOWN[1], ("c", 0, 0, 0))

        @pl.when(it == 0)
        def _():
            @pl.loop(1, LINES)
            def _(d):
                pattern_copy(d, 0).start()
                pattern_copy(d, 1).start()

        acc[...] = jnp.zeros_like(acc)
        row_e1(first)
        col_event(it, 0)
        row_fan(first, 0)
        col_event(it, 1)

        @pl.when(it == 0)
        def _():
            patterns()
            make_table(0, 8)

        row_e3(first)
        col_event(it, 2)

        @pl.when(it == 0)
        def _():
            make_table(8, 8)

        row_fan(first, -1)
        col_event(it, 3)
        row_fan(first, 1)
        col_event(it, 4)
        row_last(first, 0)
        col_event(it, 5)
        row_fan(first, 2)
        col_event(it, 6)
        row_last(first, -1, 1, 2)
        cross_wait(it, 0, 4)

        @pl.loop(0, LINES)
        def _(r):
            piece(it, first, r)

        scale = 1.0 / (2.0 * 2 * LINES * 128)
        for i in range(4):
            for t in range(2):
                block = acc[i, :, t * 128 : (t + 1) * 128]
                right[second, row, 2 * i + t] = (block * scale).astype(jnp.bfloat16)

        row_start(second)
        acc[...] = jnp.zeros_like(acc)
        row_e1(second)
        row_fan(second, 0)

        @pl.loop(0, 3)
        def _(n):
            piece(it, second, row_at(n - 1, 0))

        row_e3(second)

        @pl.loop(0, 2)
        def _(n):
            piece(it, second, row_at(0, 2 * n - 1))

        row_fan(second, -1)
        row_fan(second, 1)

        @pl.loop(0, 4)
        def _(n):
            piece(it, second, row_at(lax.div(n, 2) * 2 - 1, lax.rem(n, 2) * 2 - 1))

        row_last(second, 0)
        row_fan(second, 2)

        @pl.loop(0, 2)
        def _(n):
            piece(it, second, row_at(2 * n, 2 - 2 * n))

        row_last(second, -1, 1)

        @pl.loop(0, 2)
        def _(n):
            piece(it, second, row_at(2, 2 * n - 1))

        @pl.loop(0, 2)
        def _(n):
            piece(it, second, row_at(2 * n - 1, 2))

        row_last(second, 2)
        piece(it, second, row_at(2, 2))

        for i in range(4):
            for t in range(2):
                s = left[it, col, 2 * i + t].astype(jnp.float32)
                new = 1.5 * s - 0.5 * acc[i, :, t * 128 : (t + 1) * 128]
                keep = srow[row, i, t] >= 0
                new = jnp.where(keep, new, 0.0).astype(jnp.bfloat16)
                sign_out[i, t] = new

        @pl.when(it < ITERS - 1)
        def _():
            now = sign_out[...].reshape(BLOCKS, 128, 128)
            left[it + 1, col] = now
            right[2 * it + 2, row] = now

        for key in ROW_KEYS:
            row_copy(first, key, True).wait_send()
            row_copy(second, key, True).wait_send()
        for key in COL_KEYS:
            col_copy(it, key, True).wait_send()

    square_out[...] = right[2 * ITERS - 1, row].reshape(4, 2, 128, 128)
    for land, n in ((prow, 0), (pcol, 1)):
        some = land.at[pl.ds(0, LINES - 1)]
        pltpu.make_async_copy(some, some, psend.at[n]).wait()


def shards(tiles, pattern):
    shape = jax.ShapeDtypeStruct(tiles.shape, tiles.dtype)
    vmem = pl.BlockSpec(memory_space=pltpu.VMEM)
    dma = pltpu.SemaphoreType.DMA
    return pl.pallas_call(
        kernel,
        out_shape=(shape, shape),
        in_specs=[vmem, vmem],
        out_specs=(vmem, vmem),
        scratch_shapes=[
            pltpu.VMEM((ITERS, LINES, BLOCKS, 128, 128), jnp.bfloat16),
            pltpu.VMEM((2 * ITERS, LINES, BLOCKS, 128, 128), jnp.bfloat16),
            pltpu.VMEM((BLOCKS + 1, 128, 128), jnp.bfloat16),
            pltpu.VMEM((4, 128, 256), jnp.float32),
            pltpu.VMEM((LINES, 8, 128), jnp.int32),
            pltpu.VMEM((LINES, 8, 128), jnp.int32),
            pltpu.SMEM((LINES, 8, 128), jnp.int32),
            pltpu.SMEM((LINES, 8, 128), jnp.int32),
            pltpu.SMEM((LINES * 16,), jnp.int32),
            dma((2,)),
            dma((2,)),
            dma((2,)),
            dma((2 * ITERS, len(ROW_KEYS))),
            dma((2 * ITERS, len(ROW_KEYS))),
            dma((ITERS, len(COL_KEYS))),
            dma((ITERS, len(COL_KEYS))),
        ],
        compiler_params=pltpu.CompilerParams(
            collective_id=0, has_side_effects=True, vmem_limit_bytes=48 * 1024 * 1024
        ),
    )(tiles, pattern)


def solution(mesh):
    return jax.shard_map(
        shards,
        mesh=mesh,
        in_specs=(P("row", "col", None, None), P("row", "col")),
        out_specs=(P("row", "col", None, None), P("row", "col", None, None)),
        check_vma=False,
    )
```

```python
import jax
import jax.numpy as jnp
from jax import lax
from jax.experimental import pallas as pl
from jax.experimental.pallas import tpu as pltpu
from jax.sharding import PartitionSpec as P

ITERS = 2
SIDE = 4
RING = 8
LINES = 16
BLOCKS = 8
BS = 128
GROUP = 4
HEAD = 16
ROWS = BLOCKS * BS
MESH = pl.DeviceIdType.MESH

PARTS = {"w": (0, 4), "a": (0, 2), "b": (2, 4)}
ROW_KEYS = []
for _h in (0, 1):
    ROW_KEYS += [(_h, -1, 0, "w"), (_h, 1, 0, "w"), (_h, 2, 0, "a"), (_h, 2, 0, "b")]
    for _f in (0, -1, 1, 2):
        ROW_KEYS += [(_h, _f, -1, "w"), (_h, _f, 1, "w"), (_h, _f, 2, "a"), (_h, _f, 2, "b")]
ROW_ID = {key: n for n, key in enumerate(ROW_KEYS)}

UP = [(1, q, d) for d in (1, 2, 3) for q in (0, 1, 2, 3)] + [(1, q, 4) for q in (0, 1)]
DOWN = [(-1, q, d) for d in (1, 2, 3) for q in (2, 3, 0, 1)] + [(-1, q, 4) for q in (2, 3)]
CROSS = [("c", 1, 0)] + [("c", s, d) for d in (1, 2, 3, 4) for s in (1, -1)]
COL_ID = {key: n for n, key in enumerate(UP + DOWN + CROSS)}


def kernel(
    tiles, pattern, sign_out, square_out,
    left, right, mid, loc, acc, pv, table, used,
    tsem, psem, rsend, rrecv, csend, crecv,
):
    row, col = lax.axis_index("row"), lax.axis_index("col")
    x, y = lax.div(row, SIDE), lax.rem(row, SIDE)
    z, core = lax.div(col, 2), lax.rem(col, 2)

    def row_at(dx, dy):
        return lax.rem(x + dx + SIDE, SIDE) * SIDE + lax.rem(y + dy + SIDE, SIDE)

    def col_at(dz, own_core=True):
        return lax.rem(z + dz + RING, RING) * 2 + (core if own_core else 1 - core)

    def block(n):
        return pl.ds(HEAD + n * BS, BS)

    def row_copy(it, which, key, sending):
        h, f, s, part = key
        second = s != 0
        step = {-1: 1, 1: -1}.get(s if second else f) or (1 if part == "a" else -1)
        if sending:
            if second:
                s = s + step if s != 2 else -step
            else:
                f = f + step if f != 2 else -step
        lo, hi = ((h * 4 + p) * BS for p in PARTS[part])
        off = (f, s) if h == 0 else (s, f)
        if which == 0:
            lo, hi = lo + HEAD if lo else 0, hi + HEAD
        ref = (right, mid)[which].at[it, row_at(*off), pl.ds(lo, hi - lo)]
        target = row_at(step, 0) if (h == 0) != second else row_at(0, step)
        return pltpu.make_async_remote_copy(
            src_ref=ref, dst_ref=ref, send_sem=rsend.at[it, which], recv_sem=rrecv.at[it, which, ROW_ID[key]],
            device_id=(target, col), device_id_type=MESH,
        )

    def row_send(g, *keys):
        for key in keys:
            row_copy(*g, key, True).start()

    def row_wait(g, *keys):
        for key in keys:
            row_copy(*g, key, False).wait_recv()

    def col_copy(it, key, sending):
        sign, d = key[-3] if key[0] != "c" else key[1], key[-1]
        if key[0] == "c":
            ref_col = col_at(-sign * d, sending)
            target = col_at(0, False)
            lo, hi = (0, 4) if d < 4 else ((0, 2) if sign == 1 else (2, 4))
        else:
            ref_col = col_at(-sign * (d - 1 if sending else d))
            target = col_at(sign)
            lo, hi = key[1], key[1] + 1
        lo, hi = lo * 2 * BS + HEAD if lo else 0, hi * 2 * BS + HEAD
        ref = left.at[it, ref_col, pl.ds(lo, hi - lo)]
        return pltpu.make_async_remote_copy(
            src_ref=ref, dst_ref=ref, send_sem=csend.at[it], recv_sem=crecv.at[it, COL_ID[key]],
            device_id=(row, target), device_id_type=MESH,
        )

    def col_start(it):
        for up, down in zip(UP[:4], DOWN[:4]):
            col_copy(it, up, True).start()
            col_copy(it, down, True).start()
        col_copy(it, CROSS[0], True).start()

    def col_event(it, *ns):
        for n in ns:
            for key in (UP[n], DOWN[n]):
                col_copy(it, key, False).wait_recv()
                sign, q, d = key
                if (sign, q, d + 1) in COL_ID:
                    col_copy(it, (sign, q, d + 1), True).start()
                if n % 4 == 3 or n == 13:
                    col_copy(it, ("c", sign, d), True).start()

    def cross_wait(it, *ds):
        for key in CROSS:
            if key[2] in ds:
                col_copy(it, key, False).wait_recv()

    def row_start(g):
        for h in (0, 1):
            row_send(g, (h, -1, 0, "w"), (h, 1, 0, "w"))
        for h in (1, 0):
            row_send(g, (h, 0, -1, "w"), (h, 0, 1, "w"))

    def row_e1(g):
        for h in (0, 1):
            for f, part in ((-1, "a"), (1, "b")):
                row_wait(g, (h, f, 0, "w"))
                row_send(g, (h, 2, 0, part))
        for f in (-1, 1):
            for h in (0, 1):
                row_send(g, (h, f, -1, "w"), (h, f, 1, "w"))

    def row_e3(g):
        for h in (0, 1):
            row_wait(g, (h, 2, 0, "a"), (h, 2, 0, "b"))
            row_send(g, (h, 2, -1, "w"), (h, 2, 1, "w"))

    def row_fan(g, f):
        for h in (1, 0):
            for s, part in ((-1, "a"), (1, "b")):
                row_wait(g, (h, f, s, "w"))
                row_send(g, (h, f, 2, part))

    def row_last(g, *fs):
        for f in fs:
            for h in (0, 1):
                row_wait(g, (h, f, 2, "a"), (h, f, 2, "b"))

    def sent(ref, sem):
        some = ref.at[0, pl.ds(0, LINES - 1)]
        pltpu.make_async_copy(some, some, sem).wait()

    def pieces(it, which, rs):
        head = HEAD if which == 0 else 0
        for g, r in enumerate(rs):
            for n in range(BLOCKS):
                loc[g, n] = (right, mid)[which][it, r, pl.ds(head + n * BS, BS)]
            for i in range(4):
                a = jnp.concatenate([left[it, r, block(2 * i)], left[it, r, block(2 * i + 1)]], axis=1)
                b = [[loc[g, table[r, 4 * i + 2 * s + t]] for t in (0, 1)] for s in (0, 1)]
                b = jnp.concatenate([jnp.concatenate(pair, axis=1) for pair in b], axis=0)
                acc[i] += jnp.dot(a, b, preferred_element_type=jnp.float32)

    def apart(a, b, n):
        d = lax.rem(a - b + n, n)
        return jnp.minimum(d, n - d)

    def decode(tile):
        at = lax.broadcasted_iota(jnp.int32, (HEAD, BS), 0)
        entry = tile.astype(jnp.float32).astype(jnp.int32) + 1
        code = jnp.where(at < BLOCKS, entry << (3 * jnp.minimum(at, BLOCKS - 1)), 0)
        return jnp.sum(code, axis=0, keepdims=True)

    def make_table():
        for r in range(LINES):
            pv[0, r : r + 1] = decode(right[0, r, 0:HEAD])
            pv[1, r : r + 1] = decode(left[0, r, 0:HEAD])
        theirs, mine = pv[0], pv[1]
        own = jnp.broadcast_to(decode(left[0, col, 0:HEAD]), (LINES, BS))
        lane = lax.broadcasted_iota(jnp.int32, (LINES, BS), 1) & 15
        i, s, t = lane >> 2, (lane >> 1) & 1, lane & 1
        k = ((mine >> (6 * i + 3 * s)) & 7) - 1
        at_k = jnp.clip(k, 0, SIDE - 1)
        pair = theirs >> (6 * at_k)
        j = (own >> (6 * i + 3 * t)) & 7
        found = jnp.where((pair & 7) == j, 2 * at_k, jnp.where(((pair >> 3) & 7) == j, 2 * at_k + 1, BLOCKS))
        pv[2] = jnp.where((k >= 0) & (j > 0), found, BLOCKS)
        pv[3] = j
        copies = [pltpu.make_async_copy(pv.at[2 + n], (table, used)[n], psem.at[n]) for n in (0, 1)]
        for copy in copies:
            copy.start()
        for copy in copies:
            copy.wait()

    barrier = pltpu.get_barrier_semaphore()
    for peer in (
        (row_at(1, 0), col), (row_at(-1, 0), col), (row_at(0, 1), col), (row_at(0, -1), col),
        (row, col_at(1)), (row, col_at(-1)), (row, col_at(0, False)),
    ):
        pl.semaphore_signal(barrier, inc=1, device_id=peer, device_id_type=MESH)

    body = pl.ds(HEAD, ROWS)
    fetch = [
        pltpu.make_async_copy(tiles, right.at[0, row, body], tsem.at[0]),
        pltpu.make_async_copy(tiles, left.at[0, col, body], tsem.at[1]),
    ]
    for copy in fetch:
        copy.start()
    n_row = lax.broadcasted_iota(jnp.int32, (HEAD, BS), 0)
    head = jnp.zeros((HEAD, BS), jnp.float32)
    for n in range(BLOCKS):
        entry = jnp.broadcast_to(pattern[n % 2 : n % 2 + 1, n // 2 : n // 2 + 1], (HEAD, BS)).astype(jnp.float32)
        head = jnp.where(n_row == n, entry, head)
    for it in range(ITERS):
        right[it, row, 0:HEAD] = head.astype(jnp.bfloat16)
        left[it, col, 0:HEAD] = head.astype(jnp.bfloat16)
    for k in range(GROUP):
        loc[k, BLOCKS] = jnp.zeros((BS, BS), jnp.bfloat16)

    early, order = jnp.int32(0), [jnp.int32(0)] * (LINES // GROUP)
    for r in range(LINES):
        dx, dy, dz = apart(r // SIDE, x, SIDE), apart(r % SIDE, y, SIDE), apart(r // 2, z, RING)
        soon = jnp.where((dx + dy <= 2) & (dz <= 3), 1, 0)
        at = jnp.where(soon == 1, early, LINES - 1 - r + early)
        early = early + soon
        for k in range(LINES // GROUP):
            for j in range(GROUP):
                order[k] = order[k] + jnp.where(at == k * GROUP + j, r * 16**j, 0)

    def group(k):
        word = order[0]
        for n in range(1, LINES // GROUP):
            word = jnp.where(k == n, order[n], word)
        return [lax.rem(lax.div(word, 16**j), 16) for j in range(GROUP)]

    for copy in fetch:
        copy.wait()
    pl.semaphore_wait(barrier, 7)

    @pl.loop(0, ITERS)
    def _(it):
        g, m = (it, 0), (it, 1)

        row_start(g)
        col_start(it)
        acc[...] = jnp.zeros_like(acc)
        col_event(it, 0, 1)
        row_e1(g)
        col_event(it, 2, 3)
        row_e3(g)
        col_event(it, 4, 5, 6)
        row_fan(g, -1)
        col_event(it, 7, 8)
        row_fan(g, 1)
        col_event(it, 9, 10, 11)
        row_fan(g, 0)
        row_fan(g, 2)
        col_event(it, 12, 13)
        row_last(g, 0)
        cross_wait(it, 0, 1, 2, 3)

        @pl.when(it > 0)
        def _():
            @pl.loop(0, 2)
            def _(k):
                pieces(it, 0, group(k))

        row_last(g, -1, 1, 2)
        cross_wait(it, 4)

        @pl.when(it == 0)
        def _():
            make_table()

        @pl.loop(jnp.where(it == 0, 0, 2), 4)
        def _(k):
            pieces(it, 0, group(k))

        scale = 1.0 / (2.0 * 2 * LINES * BS)
        for i in range(4):
            for t in range(2):
                new = acc[i, :, t * BS : (t + 1) * BS] * scale
                mid[it, row, pl.ds((2 * i + t) * BS, BS)] = new.astype(jnp.bfloat16)

        row_start(m)
        acc[...] = jnp.zeros_like(acc)
        row_e1(m)
        row_e3(m)
        row_fan(m, 0)
        row_fan(m, -1)
        pieces(it, 1, [row_at(0, 0), row_at(-1, 0), row_at(1, 0)])
        row_fan(m, 1)
        pieces(it, 1, [row_at(0, -1), row_at(0, 1)])
        row_fan(m, 2)
        pieces(it, 1, [row_at(-1, -1), row_at(-1, 1), row_at(1, -1), row_at(1, 1)])
        row_last(m, 0)
        pieces(it, 1, [row_at(2, 0), row_at(0, 2)])
        for f in (-1, 1):
            row_last(m, f)
            pieces(it, 1, [row_at(2, f), row_at(f, 2)])
        row_last(m, 2)
        pieces(it, 1, [row_at(2, 2)])

        for i in range(4):
            for t in range(2):
                s = left[it, col, block(2 * i + t)].astype(jnp.float32)
                new = 1.5 * s - 0.5 * acc[i, :, t * BS : (t + 1) * BS]
                keep = used[0, 4 * i + t] > 0
                sign_out[i, t] = jnp.where(keep, new, 0.0).astype(jnp.bfloat16)

        @pl.when(it < ITERS - 1)
        def _():
            for n in range(BLOCKS):
                now = sign_out[n // 2, n % 2]
                left[it + 1, col, block(n)] = now
                right[it + 1, row, block(n)] = now

    for n in range(BLOCKS):
        square_out[n // 2, n % 2] = mid[ITERS - 1, row, pl.ds(n * BS, BS)]
    for it in range(ITERS):
        sent(right, rsend.at[it, 0])
        sent(mid, rsend.at[it, 1])
        sent(left, csend.at[it])


def shards(tiles, pattern):
    shape = jax.ShapeDtypeStruct(tiles.shape, tiles.dtype)
    vmem = pl.BlockSpec(memory_space=pltpu.VMEM)
    dma = pltpu.SemaphoreType.DMA
    return pl.pallas_call(
        kernel,
        out_shape=(shape, shape),
        in_specs=[pl.BlockSpec(memory_space=pltpu.HBM), vmem],
        out_specs=(vmem, vmem),
        scratch_shapes=[
            pltpu.VMEM((ITERS, LINES, HEAD + ROWS, BS), jnp.bfloat16),
            pltpu.VMEM((ITERS, LINES, HEAD + ROWS, BS), jnp.bfloat16),
            pltpu.VMEM((ITERS, LINES, ROWS, BS), jnp.bfloat16),
            pltpu.VMEM((GROUP, BLOCKS + 1, BS, BS), jnp.bfloat16),
            pltpu.VMEM((4, BS, 2 * BS), jnp.float32),
            pltpu.VMEM((4, LINES, BS), jnp.int32),
            pltpu.SMEM((LINES, BS), jnp.int32),
            pltpu.SMEM((LINES, BS), jnp.int32),
            dma((2,)),
            dma((2,)),
            dma((ITERS, 2)),
            dma((ITERS, 2, len(ROW_KEYS))),
            dma((ITERS,)),
            dma((ITERS, len(COL_ID))),
        ],
        compiler_params=pltpu.CompilerParams(
            collective_id=0, has_side_effects=True, vmem_limit_bytes=48 * 1024 * 1024
        ),
    )(tiles.reshape(ROWS, BS), pattern.T)


def solution(mesh):
    return jax.shard_map(
        shards,
        mesh=mesh,
        in_specs=(P("row", "col", None, None), P("row", "col")),
        out_specs=(P("row", "col", None, None), P("row", "col", None, None)),
        check_vma=False,
    )
```

```python
import jax
import jax.numpy as jnp
from jax import lax
from jax.experimental import pallas as pl
from jax.experimental.pallas import tpu as pltpu
from jax.sharding import PartitionSpec as P

ITERS = 2
SIDE = 4
RING = 8
LINES = 16
BLOCKS = 8
BS = 128
GROUP = 7
HEAD = 16
ROWS = BLOCKS * BS
MESH = pl.DeviceIdType.MESH

PARTS = {"w": (0, 4), "a": (0, 2), "b": (2, 4)}
ROW_KEYS = []
for _h in (0, 1):
    ROW_KEYS += [(_h, -1, 0, "w"), (_h, 1, 0, "w"), (_h, 2, 0, "a"), (_h, 2, 0, "b")]
    for _f in (0, -1, 1, 2):
        ROW_KEYS += [(_h, _f, -1, "w"), (_h, _f, 1, "w"), (_h, _f, 2, "a"), (_h, _f, 2, "b")]
ROW_ID = {key: n for n, key in enumerate(ROW_KEYS)}

UP = [(1, q, d) for d in (1, 2, 3) for q in (0, 1, 2, 3)] + [(1, q, 4) for q in (0, 1)]
DOWN = [(-1, q, d) for d in (1, 2, 3) for q in (2, 3, 0, 1)] + [(-1, q, 4) for q in (2, 3)]
CROSS = [("c", 1, 0)] + [("c", s, d) for d in (1, 2, 3, 4, 5) for s in (1, -1)]
COL_ID = {key: n for n, key in enumerate(UP + DOWN + CROSS)}


def kernel(
    tiles, pattern, sign_out, square_out,
    left, right, mid, loc, acc, codes, pv, table, used,
    tsem, psem, rsend, rrecv, csend, crecv,
):
    row, col = lax.axis_index("row"), lax.axis_index("col")
    x, y = lax.div(row, SIDE), lax.rem(row, SIDE)
    z, core = lax.div(col, 2), lax.rem(col, 2)

    def row_at(dx, dy):
        return lax.rem(x + dx + SIDE, SIDE) * SIDE + lax.rem(y + dy + SIDE, SIDE)

    def col_at(dz, own_core=True):
        return lax.rem(z + dz + RING, RING) * 2 + (core if own_core else 1 - core)

    def block(n):
        return pl.ds(HEAD + n * BS, BS)

    def row_copy(it, which, key, sending):
        h, f, s, part = key
        second = s != 0
        step = {-1: 1, 1: -1}.get(s if second else f) or (1 if part == "a" else -1)
        if sending:
            if second:
                s = s + step if s != 2 else -step
            else:
                f = f + step if f != 2 else -step
        lo, hi = ((h * 4 + p) * BS for p in PARTS[part])
        off = (f, s) if h == 0 else (s, f)
        if which == 0:
            lo, hi = lo + HEAD if lo else 0, hi + HEAD
        ref = (right, mid)[which].at[it, row_at(*off), pl.ds(lo, hi - lo)]
        target = row_at(step, 0) if (h == 0) != second else row_at(0, step)
        return pltpu.make_async_remote_copy(
            src_ref=ref, dst_ref=ref, send_sem=rsend.at[it, which], recv_sem=rrecv.at[it, which, ROW_ID[key]],
            device_id=(target, col), device_id_type=MESH,
        )

    def row_send(g, *keys):
        for key in keys:
            row_copy(*g, key, True).start()

    def row_wait(g, *keys):
        for key in keys:
            row_copy(*g, key, False).wait_recv()

    def col_copy(it, key, sending):
        sign, d = key[-3] if key[0] != "c" else key[1], key[-1]
        if key[0] == "c":
            ref_col = col_at(-sign * min(d, 4), sending)
            target = col_at(0, False)
            lo = d - 4 if sign == 1 else d - 2
            lo, hi = (0, 4) if d < 4 else (lo, lo + 1)
        else:
            ref_col = col_at(-sign * (d - 1 if sending else d))
            target = col_at(sign)
            lo, hi = key[1], key[1] + 1
        lo, hi = lo * 2 * BS + HEAD if lo else 0, hi * 2 * BS + HEAD
        ref = left.at[it, ref_col, pl.ds(lo, hi - lo)]
        return pltpu.make_async_remote_copy(
            src_ref=ref, dst_ref=ref, send_sem=csend.at[it], recv_sem=crecv.at[it, COL_ID[key]],
            device_id=(row, target), device_id_type=MESH,
        )

    def col_start(it):
        for up, down in zip(UP[:4], DOWN[:4]):
            col_copy(it, up, True).start()
            col_copy(it, down, True).start()
        col_copy(it, CROSS[0], True).start()

    def col_event(it, *ns):
        for n in ns:
            for key in (UP[n], DOWN[n]):
                col_copy(it, key, False).wait_recv()
                sign, q, d = key
                if (sign, q, d + 1) in COL_ID:
                    col_copy(it, (sign, q, d + 1), True).start()
                if n % 4 == 3 or n >= 12:
                    col_copy(it, ("c", sign, d + (n == 13)), True).start()

    def cross_wait(it, *ds):
        for key in CROSS:
            if key[2] in ds:
                col_copy(it, key, False).wait_recv()

    def row_start(g):
        for h in (0, 1):
            row_send(g, (h, -1, 0, "w"), (h, 1, 0, "w"))
        for h in (1, 0):
            row_send(g, (h, 0, -1, "w"), (h, 0, 1, "w"))

    def row_e1(g):
        for h in (0, 1):
            for f, part in ((-1, "a"), (1, "b")):
                row_wait(g, (h, f, 0, "w"))
                row_send(g, (h, 2, 0, part))
        for f in (-1, 1):
            for h in (0, 1):
                row_send(g, (h, f, -1, "w"), (h, f, 1, "w"))

    def row_e3(g):
        for h in (0, 1):
            row_wait(g, (h, 2, 0, "a"), (h, 2, 0, "b"))
            row_send(g, (h, 2, -1, "w"), (h, 2, 1, "w"))

    def row_fan(g, f):
        for h in (1, 0):
            for s, part in ((-1, "a"), (1, "b")):
                row_wait(g, (h, f, s, "w"))
                row_send(g, (h, f, 2, part))

    def row_last(g, *fs):
        for f in fs:
            for h in (0, 1):
                row_wait(g, (h, f, 2, "a"), (h, f, 2, "b"))

    def sent(ref, sem):
        some = ref.at[0, pl.ds(0, LINES - 1)]
        pltpu.make_async_copy(some, some, sem).wait()

    def pieces(it, which, rs):
        head = HEAD if which == 0 else 0
        for g, r in enumerate(rs):
            for n in range(BLOCKS):
                loc[g, n] = (right, mid)[which][it, r, pl.ds(head + n * BS, BS)]
            for i in range(4):
                a = jnp.concatenate([left[it, r, block(2 * i)], left[it, r, block(2 * i + 1)]], axis=1)
                b = [[loc[g, table[r, 4 * i + 2 * s + t]] for t in (0, 1)] for s in (0, 1)]
                b = jnp.concatenate([jnp.concatenate(pair, axis=1) for pair in b], axis=0)
                acc[i] += jnp.dot(a, b, preferred_element_type=jnp.float32)

    def apart(a, b, n):
        d = lax.rem(a - b + n, n)
        return jnp.minimum(d, n - d)

    def decode(tile):
        at = lax.broadcasted_iota(jnp.int32, (HEAD, BS), 0)
        weight = jnp.where(at < BLOCKS, 1 << (3 * jnp.minimum(at, BLOCKS - 1)), 0).astype(jnp.float32)
        return jnp.sum(tile.astype(jnp.float32) * weight, axis=0, keepdims=True)

    def make_table(rows, cols):
        for r in rows:
            codes[0, pl.ds(r, 1)] = decode(right[0, r, 0:HEAD])
        for c in cols:
            codes[1, pl.ds(c, 1)] = decode(left[0, c, 0:HEAD])
        ones = sum(1 << (3 * n) for n in range(BLOCKS))
        theirs, mine = codes[0].astype(jnp.int32) + ones, codes[1].astype(jnp.int32) + ones
        own = jnp.broadcast_to(decode(left[0, col, 0:HEAD]), (LINES, BS)).astype(jnp.int32) + ones
        lane = lax.broadcasted_iota(jnp.int32, (LINES, BS), 1) & 15
        i, s, t = lane >> 2, (lane >> 1) & 1, lane & 1
        k = ((mine >> (6 * i + 3 * s)) & 7) - 1
        at_k = jnp.clip(k, 0, SIDE - 1)
        pair = theirs >> (6 * at_k)
        j = (own >> (6 * i + 3 * t)) & 7
        found = jnp.where((pair & 7) == j, 2 * at_k, jnp.where(((pair >> 3) & 7) == j, 2 * at_k + 1, BLOCKS))
        pv[0] = jnp.where((k >= 0) & (j > 0), found, BLOCKS)
        pv[1] = j
        copies = [pltpu.make_async_copy(pv.at[n], (table, used)[n], psem.at[n]) for n in (0, 1)]
        for copy in copies:
            copy.start()
        for copy in copies:
            copy.wait()

    def order_pieces():
        ranks = []
        for r in range(LINES):
            dx, dy, dz = apart(r // SIDE, x, SIDE), apart(r % SIDE, y, SIDE), apart(r // 2, z, RING)
            mine = core == r % 2
            soon = (dx + dy <= 2) & ((dz <= 2) | (mine & (dz <= 3)))
            later = (dx + dy <= 3) & ((dz <= 2) | mine)
            ranks.append((soon.astype(jnp.int32), later.astype(jnp.int32)))
        first, second, third = jnp.int32(0), sum(soon for soon, _ in ranks), jnp.int32(LINES - 1)
        order = [jnp.int32(0)] * 4
        for r, (soon, later) in enumerate(ranks):
            at = jnp.where(soon == 1, first, jnp.where(later == 1, second, third))
            first, second, third = first + soon, second + later - soon, third - (1 - later)
            for n in range(LINES):
                order[n // 4] = order[n // 4] + jnp.where(at == n, r * 16 ** (n % 4), 0)
        return [lax.rem(lax.div(order[n // 4], 16 ** (n % 4)), 16) for n in range(LINES)]

    barrier = pltpu.get_barrier_semaphore()
    for peer in (
        (row_at(1, 0), col), (row_at(-1, 0), col), (row_at(0, 1), col), (row_at(0, -1), col),
        (row, col_at(1)), (row, col_at(-1)), (row, col_at(0, False)),
    ):
        pl.semaphore_signal(barrier, inc=1, device_id=peer, device_id_type=MESH)

    body = pl.ds(HEAD, ROWS)
    fetch = [
        pltpu.make_async_copy(tiles, right.at[0, row, body], tsem.at[0]),
        pltpu.make_async_copy(tiles, left.at[0, col, body], tsem.at[1]),
    ]
    for copy in fetch:
        copy.start()
    n_row = lax.broadcasted_iota(jnp.int32, (HEAD, BS), 0)
    head = jnp.zeros((HEAD, BS), jnp.float32)
    for n in range(BLOCKS):
        entry = jnp.broadcast_to(pattern[n % 2 : n % 2 + 1, n // 2 : n // 2 + 1], (HEAD, BS)).astype(jnp.float32)
        head = jnp.where(n_row == n, entry, head)
    right[0, row, 0:HEAD] = head.astype(jnp.bfloat16)
    left[0, col, 0:HEAD] = head.astype(jnp.bfloat16)
    for copy in fetch:
        copy.wait()
    pl.semaphore_wait(barrier, 7)

    @pl.loop(0, ITERS)
    def _(it):
        g, m = (it, 0), (it, 1)

        row_start(g)
        col_start(it)
        acc[...] = jnp.zeros_like(acc)
        order = order_pieces()

        @pl.when(it == 0)
        def _():
            codes[...] = jnp.zeros_like(codes)
            for k in range(GROUP):
                loc[k, BLOCKS] = jnp.zeros((BS, BS), jnp.bfloat16)
            right[1, row, 0:HEAD] = right[0, row, 0:HEAD]
            left[1, col, 0:HEAD] = left[0, col, 0:HEAD]

        col_event(it, 0, 1)
        row_e1(g)
        col_event(it, 2, 3)
        row_e3(g)
        col_event(it, 4, 5, 6)
        row_fan(g, 0)
        row_fan(g, -1)
        col_event(it, 7, 8)
        row_fan(g, 1)
        col_event(it, 9, 10, 11)
        row_fan(g, 2)
        row_last(g, 0)
        cross_wait(it, 0, 1, 2)

        @pl.when(it == 0)
        def _():
            make_table(
                [row_at(dx, dy) for dx in (-1, 0, 1, 2) for dy in (-1, 0, 1, 2) if abs(dx) + abs(dy) <= 2],
                [col_at(dz) for dz in range(-3, 4)] + [col_at(dz, False) for dz in range(-2, 3)],
            )

        pieces(it, 0, order[:7])
        col_event(it, 12)
        row_last(g, -1)
        col_event(it, 13)
        row_last(g, 1)

        @pl.when(it == 0)
        def _():
            make_table([row_at(2, -1), row_at(2, 1), row_at(-1, 2), row_at(1, 2)], [col_at(4)])

        pieces(it, 0, order[7:12])
        row_last(g, 2)
        cross_wait(it, 3, 4, 5)

        @pl.when(it == 0)
        def _():
            make_table([row_at(2, 2)], [col_at(dz, False) for dz in (-3, 3, 4)])

        pieces(it, 0, order[12:])

        scale = 1.0 / (2.0 * 2 * LINES * BS)
        for i in range(4):
            for t in range(2):
                new = (acc[i, :, t * BS : (t + 1) * BS] * scale).astype(jnp.bfloat16)
                mid[it, row, pl.ds((2 * i + t) * BS, BS)] = new
                square_out[i, t] = new

        row_start(m)
        acc[...] = jnp.zeros_like(acc)
        row_e1(m)
        row_e3(m)
        row_fan(m, 0)
        row_fan(m, -1)
        pieces(it, 1, [row_at(0, 0), row_at(-1, 0), row_at(1, 0)])
        row_fan(m, 1)
        pieces(it, 1, [row_at(0, -1), row_at(0, 1)])
        row_fan(m, 2)
        pieces(it, 1, [row_at(-1, -1), row_at(-1, 1), row_at(1, -1), row_at(1, 1)])
        row_last(m, 0)
        pieces(it, 1, [row_at(2, 0), row_at(0, 2)])
        for f in (-1, 1):
            row_last(m, f)
            pieces(it, 1, [row_at(2, f), row_at(f, 2)])
        row_last(m, 2)
        pieces(it, 1, [row_at(2, 2)])

        def new_sign(i, t):
            s = left[it, col, block(2 * i + t)].astype(jnp.float32)
            new = 1.5 * s - 0.5 * acc[i, :, t * BS : (t + 1) * BS]
            return jnp.where(used[0, 4 * i + t] > 0, new, 0.0).astype(jnp.bfloat16)

        @pl.when(it < ITERS - 1)
        def _():
            for n in range(BLOCKS):
                now = new_sign(n // 2, n % 2)
                right[it + 1, row, block(n)] = now
                left[it + 1, col, block(n)] = now

        @pl.when(it == ITERS - 1)
        def _():
            for n in range(BLOCKS):
                sign_out[n // 2, n % 2] = new_sign(n // 2, n % 2)

    for it in range(ITERS):
        sent(right, rsend.at[it, 0])
        sent(mid, rsend.at[it, 1])
        sent(left, csend.at[it])


def shards(tiles, pattern):
    shape = jax.ShapeDtypeStruct(tiles.shape, tiles.dtype)
    vmem = pl.BlockSpec(memory_space=pltpu.VMEM)
    dma = pltpu.SemaphoreType.DMA
    return pl.pallas_call(
        kernel,
        out_shape=(shape, shape),
        in_specs=[pl.BlockSpec(memory_space=pltpu.HBM), vmem],
        out_specs=(vmem, vmem),
        scratch_shapes=[
            pltpu.VMEM((ITERS, LINES, HEAD + ROWS, BS), jnp.bfloat16),
            pltpu.VMEM((ITERS, LINES, HEAD + ROWS, BS), jnp.bfloat16),
            pltpu.VMEM((ITERS, LINES, ROWS, BS), jnp.bfloat16),
            pltpu.VMEM((GROUP, BLOCKS + 1, BS, BS), jnp.bfloat16),
            pltpu.VMEM((4, BS, 2 * BS), jnp.float32),
            pltpu.VMEM((2, LINES, BS), jnp.float32),
            pltpu.VMEM((2, LINES, BS), jnp.int32),
            pltpu.SMEM((LINES, BS), jnp.int32),
            pltpu.SMEM((LINES, BS), jnp.int32),
            dma((2,)),
            dma((2,)),
            dma((ITERS, 2)),
            dma((ITERS, 2, len(ROW_KEYS))),
            dma((ITERS,)),
            dma((ITERS, len(COL_ID))),
        ],
        compiler_params=pltpu.CompilerParams(
            collective_id=0, has_side_effects=True, vmem_limit_bytes=48 * 1024 * 1024
        ),
    )(tiles.reshape(ROWS, BS), pattern.T)


def solution(mesh):
    return jax.shard_map(
        shards,
        mesh=mesh,
        in_specs=(P("row", "col", None, None), P("row", "col")),
        out_specs=(P("row", "col", None, None), P("row", "col", None, None)),
        check_vma=False,
    )
```

```python
import jax
import jax.numpy as jnp
from jax import lax
from jax.experimental import pallas as pl
from jax.experimental.pallas import tpu as pltpu
from jax.sharding import PartitionSpec as P

ITERS = 2
SIDE = 4
RING = 8
LINES = 16
BLOCKS = 8
BS = 128
GROUP = 7
HEAD = 16
ROWS = BLOCKS * BS
MESH = pl.DeviceIdType.MESH

PARTS = {"w": (0, 4), "a": (0, 2), "b": (2, 4)}
ROW_KEYS = []
for _h in (0, 1):
    ROW_KEYS += [(_h, -1, 0, "w"), (_h, 1, 0, "w"), (_h, 2, 0, "a"), (_h, 2, 0, "b")]
    for _f in (0, -1, 1, 2):
        ROW_KEYS += [(_h, _f, -1, "w"), (_h, _f, 1, "w"), (_h, _f, 2, "a"), (_h, _f, 2, "b")]
ROW_ID = {key: n for n, key in enumerate(ROW_KEYS)}

UP = [(1, q, d) for d in (1, 2, 3) for q in (0, 1, 2, 3)] + [(1, q, 4) for q in (0, 1)]
DOWN = [(-1, q, d) for d in (1, 2, 3) for q in (2, 3, 0, 1)] + [(-1, q, 4) for q in (2, 3)]
CROSS = [("c", 1, 0)] + [("c", s, d) for d in (1, 2, 3, 4, 5) for s in (1, -1)]
COL_ID = {key: n for n, key in enumerate(UP + DOWN + CROSS)}


def kernel(
    tiles, pattern, out,
    left, right, mid, loc, acc, codes, pv, table, used,
    tsem, psem, rsend, rrecv, csend, crecv,
):
    sign_out, square_out = out.at[0], out.at[1]
    row, col = lax.axis_index("row"), lax.axis_index("col")
    x, y = lax.div(row, SIDE), lax.rem(row, SIDE)
    z, core = lax.div(col, 2), lax.rem(col, 2)

    def row_at(dx, dy):
        return lax.rem(x + dx + SIDE, SIDE) * SIDE + lax.rem(y + dy + SIDE, SIDE)

    def col_at(dz, own_core=True):
        return lax.rem(z + dz + RING, RING) * 2 + (core if own_core else 1 - core)

    def block(n):
        return pl.ds(HEAD + n * BS, BS)

    def row_copy(it, which, key, sending):
        h, f, s, part = key
        second = s != 0
        step = {-1: 1, 1: -1}.get(s if second else f) or (1 if part == "a" else -1)
        if sending:
            if second:
                s = s + step if s != 2 else -step
            else:
                f = f + step if f != 2 else -step
        lo, hi = ((h * 4 + p) * BS for p in PARTS[part])
        off = (f, s) if h == 0 else (s, f)
        if which == 0:
            lo, hi = lo + HEAD if lo else 0, hi + HEAD
        ref = (right, mid)[which].at[it, row_at(*off), pl.ds(lo, hi - lo)]
        target = row_at(step, 0) if (h == 0) != second else row_at(0, step)
        return pltpu.make_async_remote_copy(
            src_ref=ref, dst_ref=ref, send_sem=rsend.at[it, which], recv_sem=rrecv.at[it, which, ROW_ID[key]],
            device_id=(target, col), device_id_type=MESH,
        )

    def row_send(g, *keys):
        for key in keys:
            row_copy(*g, key, True).start()

    def row_wait(g, *keys):
        for key in keys:
            row_copy(*g, key, False).wait_recv()

    def col_copy(it, key, sending):
        sign, d = key[-3] if key[0] != "c" else key[1], key[-1]
        if key[0] == "c":
            ref_col = col_at(-sign * min(d, 4), sending)
            target = col_at(0, False)
            lo = d - 4 if sign == 1 else d - 2
            lo, hi = (0, 4) if d < 4 else (lo, lo + 1)
        else:
            ref_col = col_at(-sign * (d - 1 if sending else d))
            target = col_at(sign)
            lo, hi = key[1], key[1] + 1
        lo, hi = lo * 2 * BS + HEAD if lo else 0, hi * 2 * BS + HEAD
        ref = left.at[it, ref_col, pl.ds(lo, hi - lo)]
        return pltpu.make_async_remote_copy(
            src_ref=ref, dst_ref=ref, send_sem=csend.at[it], recv_sem=crecv.at[it, COL_ID[key]],
            device_id=(row, target), device_id_type=MESH,
        )

    def col_start(it):
        for up, down in zip(UP[:4], DOWN[:4]):
            col_copy(it, up, True).start()
            col_copy(it, down, True).start()
        col_copy(it, CROSS[0], True).start()

    def col_event(it, *ns):
        for n in ns:
            for key in (UP[n], DOWN[n]):
                col_copy(it, key, False).wait_recv()
                sign, q, d = key
                if (sign, q, d + 1) in COL_ID:
                    col_copy(it, (sign, q, d + 1), True).start()
                if n % 4 == 3 or n >= 12:
                    col_copy(it, ("c", sign, d + (n == 13)), True).start()

    def cross_wait(it, *ds):
        for key in CROSS:
            if key[2] in ds:
                col_copy(it, key, False).wait_recv()

    def row_start(g):
        for h in (0, 1):
            row_send(g, (h, -1, 0, "w"), (h, 1, 0, "w"))
        for h in (1, 0):
            row_send(g, (h, 0, -1, "w"), (h, 0, 1, "w"))

    def row_e1(g):
        for h in (0, 1):
            for f, part in ((-1, "a"), (1, "b")):
                row_wait(g, (h, f, 0, "w"))
                row_send(g, (h, 2, 0, part))
        for f in (-1, 1):
            for h in (0, 1):
                row_send(g, (h, f, -1, "w"), (h, f, 1, "w"))

    def row_e3(g):
        for h in (0, 1):
            row_wait(g, (h, 2, 0, "a"), (h, 2, 0, "b"))
            row_send(g, (h, 2, -1, "w"), (h, 2, 1, "w"))

    def row_fan(g, f):
        for h in (1, 0):
            for s, part in ((-1, "a"), (1, "b")):
                row_wait(g, (h, f, s, "w"))
                row_send(g, (h, f, 2, part))

    def row_last(g, *fs):
        for f in fs:
            for h in (0, 1):
                row_wait(g, (h, f, 2, "a"), (h, f, 2, "b"))

    def sent(ref, sem):
        some = ref.at[0, pl.ds(0, LINES - 1)]
        pltpu.make_async_copy(some, some, sem).wait()

    def pieces(it, which, rs):
        head = HEAD if which == 0 else 0
        for g, r in enumerate(rs):
            for n in range(BLOCKS):
                loc[g, n] = (right, mid)[which][it, r, pl.ds(head + n * BS, BS)]
            for i in range(4):
                a = jnp.concatenate([left[it, r, block(2 * i)], left[it, r, block(2 * i + 1)]], axis=1)
                b = [[loc[g, table[r, 4 * i + 2 * s + t]] for t in (0, 1)] for s in (0, 1)]
                b = jnp.concatenate([jnp.concatenate(pair, axis=1) for pair in b], axis=0)
                acc[i] += jnp.dot(a, b, preferred_element_type=jnp.float32)

    def apart(a, b, n):
        d = lax.rem(a - b + n, n)
        return jnp.minimum(d, n - d)

    def decode(tile):
        at = lax.broadcasted_iota(jnp.int32, (HEAD, BS), 0)
        weight = jnp.where(at < BLOCKS, 1 << (3 * jnp.minimum(at, BLOCKS - 1)), 0).astype(jnp.float32)
        return jnp.sum(tile.astype(jnp.float32) * weight, axis=0, keepdims=True)

    def make_table(rows, cols):
        for r in rows:
            codes[0, pl.ds(r, 1)] = decode(right[0, r, 0:HEAD])
        for c in cols:
            codes[1, pl.ds(c, 1)] = decode(left[0, c, 0:HEAD])
        ones = sum(1 << (3 * n) for n in range(BLOCKS))
        theirs, mine = codes[0].astype(jnp.int32) + ones, codes[1].astype(jnp.int32) + ones
        own = jnp.broadcast_to(decode(left[0, col, 0:HEAD]), (LINES, BS)).astype(jnp.int32) + ones
        lane = lax.broadcasted_iota(jnp.int32, (LINES, BS), 1) & 15
        i, s, t = lane >> 2, (lane >> 1) & 1, lane & 1
        k = ((mine >> (6 * i + 3 * s)) & 7) - 1
        at_k = jnp.clip(k, 0, SIDE - 1)
        pair = theirs >> (6 * at_k)
        j = (own >> (6 * i + 3 * t)) & 7
        found = jnp.where((pair & 7) == j, 2 * at_k, jnp.where(((pair >> 3) & 7) == j, 2 * at_k + 1, BLOCKS))
        pv[0] = jnp.where((k >= 0) & (j > 0), found, BLOCKS)
        pv[1] = j
        copies = [pltpu.make_async_copy(pv.at[n], (table, used)[n], psem.at[n]) for n in (0, 1)]
        for copy in copies:
            copy.start()
        for copy in copies:
            copy.wait()

    def order_pieces():
        ranks = []
        for r in range(LINES):
            dx, dy, dz = apart(r // SIDE, x, SIDE), apart(r % SIDE, y, SIDE), apart(r // 2, z, RING)
            mine = core == r % 2
            soon = (dx + dy <= 2) & ((dz <= 2) | (mine & (dz <= 3)))
            later = (dx + dy <= 3) & ((dz <= 2) | mine)
            ranks.append((soon.astype(jnp.int32), later.astype(jnp.int32)))
        first, second, third = jnp.int32(0), sum(soon for soon, _ in ranks), jnp.int32(LINES - 1)
        order = [jnp.int32(0)] * 4
        for r, (soon, later) in enumerate(ranks):
            at = jnp.where(soon == 1, first, jnp.where(later == 1, second, third))
            first, second, third = first + soon, second + later - soon, third - (1 - later)
            for n in range(LINES):
                order[n // 4] = order[n // 4] + jnp.where(at == n, r * 16 ** (n % 4), 0)
        return [lax.rem(lax.div(order[n // 4], 16 ** (n % 4)), 16) for n in range(LINES)]

    barrier = pltpu.get_barrier_semaphore()
    for peer in (
        (row_at(1, 0), col), (row_at(-1, 0), col), (row_at(0, 1), col), (row_at(0, -1), col),
        (row, col_at(1)), (row, col_at(-1)), (row, col_at(0, False)),
    ):
        pl.semaphore_signal(barrier, inc=1, device_id=peer, device_id_type=MESH)

    body = pl.ds(HEAD, ROWS)
    fetch = [
        pltpu.make_async_copy(tiles, right.at[0, row, body], tsem.at[0]),
        pltpu.make_async_copy(tiles, left.at[0, col, body], tsem.at[1]),
    ]
    for copy in fetch:
        copy.start()
    n_row = lax.broadcasted_iota(jnp.int32, (HEAD, BS), 0)
    head = jnp.zeros((HEAD, BS), jnp.float32)
    for n in range(BLOCKS):
        entry = jnp.broadcast_to(pattern[n % 2 : n % 2 + 1, n // 2 : n // 2 + 1], (HEAD, BS)).astype(jnp.float32)
        head = jnp.where(n_row == n, entry, head)
    right[0, row, 0:HEAD] = head.astype(jnp.bfloat16)
    left[0, col, 0:HEAD] = head.astype(jnp.bfloat16)
    for copy in fetch:
        copy.wait()
    pl.semaphore_wait(barrier, 7)

    @pl.loop(0, ITERS)
    def _(it):
        g, m = (it, 0), (it, 1)

        row_start(g)
        col_start(it)
        acc[...] = jnp.zeros_like(acc)
        order = order_pieces()

        @pl.when(it == 0)
        def _():
            codes[...] = jnp.zeros_like(codes)
            for k in range(GROUP):
                loc[k, BLOCKS] = jnp.zeros((BS, BS), jnp.bfloat16)
            right[1, row, 0:HEAD] = right[0, row, 0:HEAD]
            left[1, col, 0:HEAD] = left[0, col, 0:HEAD]

        col_event(it, 0,1)
        row_e1(g)
        col_event(it, 2,3)
        row_fan(g, 0)
        row_e3(g)
        col_event(it, 4,5,6)
        row_fan(g, -1)
        col_event(it, 7,8)
        row_fan(g, 1)
        col_event(it, 9,10,11)
        row_fan(g, 2)
        row_last(g, 0)
        cross_wait(it, 0,1,2)

        @pl.when(it == 0)
        def _():
            make_table(
                [row_at(dx, dy) for dx in (-1, 0, 1, 2) for dy in (-1, 0, 1, 2) if abs(dx) + abs(dy) <= 2],
                [col_at(dz) for dz in range(-3, 4)] + [col_at(dz, False) for dz in range(-2, 3)],
            )

        col_event(it, 12)
        pieces(it, 0, order[:7])
        row_last(g, -1)
        col_event(it, 13)
        row_last(g, 1)

        @pl.when(it == 0)
        def _():
            make_table([row_at(2, -1), row_at(2, 1), row_at(-1, 2), row_at(1, 2)], [col_at(4)])

        pieces(it, 0, order[7:12])
        row_last(g, 2)
        cross_wait(it, 3, 4, 5)

        @pl.when(it == 0)
        def _():
            make_table([row_at(2, 2)], [col_at(dz, False) for dz in (-3, 3, 4)])

        pieces(it, 0, order[12:])

        scale = 1.0 / (2.0 * 2 * LINES * BS)
        for i in range(4):
            for t in range(2):
                new = (acc[i, :, t * BS : (t + 1) * BS] * scale).astype(jnp.bfloat16)
                mid[it, row, pl.ds((2 * i + t) * BS, BS)] = new
                square_out[i, t] = new

        row_start(m)
        acc[...] = jnp.zeros_like(acc)
        row_e1(m)
        row_e3(m)
        row_fan(m, 0)
        row_fan(m, -1)
        pieces(it, 1, [row_at(0, 0), row_at(-1, 0), row_at(1, 0)])
        row_fan(m, 1)
        pieces(it, 1, [row_at(0, -1), row_at(0, 1)])
        row_fan(m, 2)
        pieces(it, 1, [row_at(-1, -1), row_at(-1, 1), row_at(1, -1), row_at(1, 1)])
        row_last(m, 0)
        pieces(it, 1, [row_at(2, 0), row_at(0, 2)])
        for f in (-1, 1):
            row_last(m, f)
            pieces(it, 1, [row_at(2, f), row_at(f, 2)])
        row_last(m, 2)
        pieces(it, 1, [row_at(2, 2)])

        def new_sign(i, t):
            s = left[it, col, block(2 * i + t)].astype(jnp.float32)
            new = 1.5 * s - 0.5 * acc[i, :, t * BS : (t + 1) * BS]
            return jnp.where(used[0, 4 * i + t] > 0, new, 0.0).astype(jnp.bfloat16)

        @pl.when(it < ITERS - 1)
        def _():
            for n in range(BLOCKS):
                now = new_sign(n // 2, n % 2)
                right[it + 1, row, block(n)] = now
                left[it + 1, col, block(n)] = now

        @pl.when(it == ITERS - 1)
        def _():
            for n in range(BLOCKS):
                sign_out[n // 2, n % 2] = new_sign(n // 2, n % 2)

    for it in range(ITERS):
        sent(right, rsend.at[it, 0])
        sent(mid, rsend.at[it, 1])
        sent(left, csend.at[it])


def shards(tiles, pattern):
    shape = jax.ShapeDtypeStruct(tiles.shape, tiles.dtype)
    vmem = pl.BlockSpec(memory_space=pltpu.VMEM)
    dma = pltpu.SemaphoreType.DMA
    both = pl.pallas_call(
        kernel,
        out_shape=jax.ShapeDtypeStruct((2,) + tiles.shape, tiles.dtype),
        in_specs=[pl.BlockSpec(memory_space=pltpu.HBM), vmem],
        out_specs=vmem,
        scratch_shapes=[
            pltpu.VMEM((ITERS, LINES, HEAD + ROWS, BS), jnp.bfloat16),
            pltpu.VMEM((ITERS, LINES, HEAD + ROWS, BS), jnp.bfloat16),
            pltpu.VMEM((ITERS, LINES, ROWS, BS), jnp.bfloat16),
            pltpu.VMEM((GROUP, BLOCKS + 1, BS, BS), jnp.bfloat16),
            pltpu.VMEM((4, BS, 2 * BS), jnp.float32),
            pltpu.VMEM((2, LINES, BS), jnp.float32),
            pltpu.VMEM((2, LINES, BS), jnp.int32),
            pltpu.SMEM((LINES, BS), jnp.int32),
            pltpu.SMEM((LINES, BS), jnp.int32),
            dma((2,)),
            dma((2,)),
            dma((ITERS, 2)),
            dma((ITERS, 2, len(ROW_KEYS))),
            dma((ITERS,)),
            dma((ITERS, len(COL_ID))),
        ],
        compiler_params=pltpu.CompilerParams(
            collective_id=0, has_side_effects=True, vmem_limit_bytes=48 * 1024 * 1024
        ),
    )(tiles.reshape(ROWS, BS), pattern.T)
    return both[0], both[1]


def solution(mesh):
    return jax.shard_map(
        shards,
        mesh=mesh,
        in_specs=(P("row", "col", None, None), P("row", "col")),
        out_specs=(P("row", "col", None, None), P("row", "col", None, None)),
        check_vma=False,
    )
```

```python
import jax
import jax.numpy as jnp
from jax import lax
from jax.experimental import pallas as pl
from jax.experimental.pallas import tpu as pltpu
from jax.sharding import PartitionSpec as P

ITERS = 2
SIDE = 4
RING = 8
LINES = 16
BLOCKS = 8
BS = 128
GROUP = 7
HEAD = 16
ROWS = BLOCKS * BS
MESH = pl.DeviceIdType.MESH

PARTS = {"w": (0, 4), "a": (0, 2), "b": (2, 4)}
ROW_KEYS = []
for _h in (0, 1):
    ROW_KEYS += [(_h, -1, 0, "w"), (_h, 1, 0, "w"), (_h, 2, 0, "a"), (_h, 2, 0, "b")]
    for _f in (0, -1, 1, 2):
        ROW_KEYS += [(_h, _f, -1, "w"), (_h, _f, 1, "w"), (_h, _f, 2, "a"), (_h, _f, 2, "b")]
ROW_ID = {key: n for n, key in enumerate(ROW_KEYS)}

UP = [(1, q, d) for d in (1, 2, 3) for q in (0, 1, 2, 3)] + [(1, q, 4) for q in (0, 1)]
DOWN = [(-1, q, d) for d in (1, 2, 3) for q in (2, 3, 0, 1)] + [(-1, q, 4) for q in (2, 3)]
CROSS = [("c", 1, 0)] + [("c", s, d) for d in (1, 2, 3, 4, 5) for s in (1, -1)]
COL_ID = {key: n for n, key in enumerate(UP + DOWN + CROSS)}


def kernel(
    tiles, pattern, out,
    left, right, mid, loc, acc, codes, pv, table, used,
    tsem, psem, rsend, rrecv, csend, crecv,
):
    sign_out, square_out = out.at[0], out.at[1]
    row, col = lax.axis_index("row"), lax.axis_index("col")
    x, y = lax.div(row, SIDE), lax.rem(row, SIDE)
    z, core = lax.div(col, 2), lax.rem(col, 2)

    def row_at(dx, dy):
        return lax.rem(x + dx + SIDE, SIDE) * SIDE + lax.rem(y + dy + SIDE, SIDE)

    def col_at(dz, own_core=True):
        return lax.rem(z + dz + RING, RING) * 2 + (core if own_core else 1 - core)

    def block(n):
        return pl.ds(HEAD + n * BS, BS)

    def row_copy(it, which, key, sending):
        h, f, s, part = key
        second = s != 0
        step = {-1: 1, 1: -1}.get(s if second else f) or (1 if part == "a" else -1)
        if sending:
            if second:
                s = s + step if s != 2 else -step
            else:
                f = f + step if f != 2 else -step
        lo, hi = ((h * 4 + p) * BS for p in PARTS[part])
        off = (f, s) if h == 0 else (s, f)
        if which == 0:
            lo, hi = lo + HEAD if lo else 0, hi + HEAD
        ref = (right, mid)[which].at[it, row_at(*off), pl.ds(lo, hi - lo)]
        target = row_at(step, 0) if (h == 0) != second else row_at(0, step)
        return pltpu.make_async_remote_copy(
            src_ref=ref, dst_ref=ref, send_sem=rsend.at[it, which], recv_sem=rrecv.at[it, which, ROW_ID[key]],
            device_id=(target, col), device_id_type=MESH,
        )

    def row_send(g, *keys):
        for key in keys:
            row_copy(*g, key, True).start()

    def row_wait(g, *keys):
        for key in keys:
            row_copy(*g, key, False).wait_recv()

    def col_copy(it, key, sending):
        sign, d = key[-3] if key[0] != "c" else key[1], key[-1]
        if key[0] == "c":
            ref_col = col_at(-sign * min(d, 4), sending)
            target = col_at(0, False)
            lo = d - 4 if sign == 1 else d - 2
            lo, hi = (0, 4) if d < 4 else (lo, lo + 1)
        else:
            ref_col = col_at(-sign * (d - 1 if sending else d))
            target = col_at(sign)
            lo, hi = key[1], key[1] + 1
        lo, hi = lo * 2 * BS + HEAD if lo else 0, hi * 2 * BS + HEAD
        ref = left.at[it, ref_col, pl.ds(lo, hi - lo)]
        return pltpu.make_async_remote_copy(
            src_ref=ref, dst_ref=ref, send_sem=csend.at[it], recv_sem=crecv.at[it, COL_ID[key]],
            device_id=(row, target), device_id_type=MESH,
        )

    def col_start(it):
        for up, down in zip(UP[:4], DOWN[:4]):
            col_copy(it, up, True).start()
            col_copy(it, down, True).start()
        col_copy(it, CROSS[0], True).start()

    def col_event(it, *ns):
        for n in ns:
            for key in (UP[n], DOWN[n]):
                col_copy(it, key, False).wait_recv()
                sign, q, d = key
                if (sign, q, d + 1) in COL_ID:
                    col_copy(it, (sign, q, d + 1), True).start()
                if n % 4 == 3 or n >= 12:
                    col_copy(it, ("c", sign, d + (n == 13)), True).start()

    def cross_wait(it, *ds):
        for key in CROSS:
            if key[2] in ds:
                col_copy(it, key, False).wait_recv()

    def row_start(g, ready=lambda h: None):
        for h in (0, 1):
            ready(h)
            row_send(g, (h, -1, 0, "w"), (h, 1, 0, "w"))
        for h in (1, 0):
            row_send(g, (h, 0, -1, "w"), (h, 0, 1, "w"))

    def row_e1(g):
        for h in (0, 1):
            for f, part in ((-1, "a"), (1, "b")):
                row_wait(g, (h, f, 0, "w"))
                row_send(g, (h, 2, 0, part))
        for f in (-1, 1):
            for h in (0, 1):
                row_send(g, (h, f, -1, "w"), (h, f, 1, "w"))

    def row_e3(g):
        for h in (0, 1):
            row_wait(g, (h, 2, 0, "a"), (h, 2, 0, "b"))
            row_send(g, (h, 2, -1, "w"), (h, 2, 1, "w"))

    def row_fan(g, f):
        for h in (1, 0):
            for s, part in ((-1, "a"), (1, "b")):
                row_wait(g, (h, f, s, "w"))
                row_send(g, (h, f, 2, part))

    def row_last(g, *fs):
        for f in fs:
            for h in (0, 1):
                row_wait(g, (h, f, 2, "a"), (h, f, 2, "b"))

    def sent(ref, sem):
        some = ref.at[0, pl.ds(0, LINES - 1)]
        pltpu.make_async_copy(some, some, sem).wait()

    def pieces(it, which, rs):
        head = HEAD if which == 0 else 0
        for g, r in enumerate(rs):
            for n in range(BLOCKS):
                loc[g, n] = (right, mid)[which][it, r, pl.ds(head + n * BS, BS)]
            for i in range(4):
                a = jnp.concatenate([left[it, r, block(2 * i)], left[it, r, block(2 * i + 1)]], axis=1)
                b = [[loc[g, table[r, 4 * i + 2 * s + t]] for t in (0, 1)] for s in (0, 1)]
                b = jnp.concatenate([jnp.concatenate(pair, axis=1) for pair in b], axis=0)
                acc[i] += jnp.dot(a, b, preferred_element_type=jnp.float32)

    def apart(a, b, n):
        d = lax.rem(a - b + n, n)
        return jnp.minimum(d, n - d)

    def decode(tile):
        at = lax.broadcasted_iota(jnp.int32, (HEAD, BS), 0)
        weight = jnp.where(at < BLOCKS, 1 << (3 * jnp.minimum(at, BLOCKS - 1)), 0).astype(jnp.float32)
        return jnp.sum(tile.astype(jnp.float32) * weight, axis=0, keepdims=True)

    def make_table(rows, cols):
        for r in rows:
            codes[0, pl.ds(r, 1)] = decode(right[0, r, 0:HEAD])
        for c in cols:
            codes[1, pl.ds(c, 1)] = decode(left[0, c, 0:HEAD])
        ones = sum(1 << (3 * n) for n in range(BLOCKS))
        theirs, mine = codes[0].astype(jnp.int32) + ones, codes[1].astype(jnp.int32) + ones
        own = jnp.broadcast_to(decode(left[0, col, 0:HEAD]), (LINES, BS)).astype(jnp.int32) + ones
        lane = lax.broadcasted_iota(jnp.int32, (LINES, BS), 1) & 15
        i, s, t = lane >> 2, (lane >> 1) & 1, lane & 1
        k = ((mine >> (6 * i + 3 * s)) & 7) - 1
        at_k = jnp.clip(k, 0, SIDE - 1)
        pair = theirs >> (6 * at_k)
        j = (own >> (6 * i + 3 * t)) & 7
        found = jnp.where((pair & 7) == j, 2 * at_k, jnp.where(((pair >> 3) & 7) == j, 2 * at_k + 1, BLOCKS))
        pv[0] = jnp.where((k >= 0) & (j > 0), found, BLOCKS)
        pv[1] = j
        copies = [pltpu.make_async_copy(pv.at[n], (table, used)[n], psem.at[n]) for n in (0, 1)]
        for copy in copies:
            copy.start()
        for copy in copies:
            copy.wait()

    def order_pieces():
        ranks = []
        for r in range(LINES):
            dx, dy, dz = apart(r // SIDE, x, SIDE), apart(r % SIDE, y, SIDE), apart(r // 2, z, RING)
            mine = core == r % 2
            soon = (dx + dy <= 2) & ((dz <= 2) | (mine & (dz <= 3)))
            later = (dx + dy <= 3) & ((dz <= 2) | mine)
            ranks.append((soon.astype(jnp.int32), later.astype(jnp.int32)))
        first, second, third = jnp.int32(0), sum(soon for soon, _ in ranks), jnp.int32(LINES - 1)
        order = [jnp.int32(0)] * 4
        for r, (soon, later) in enumerate(ranks):
            at = jnp.where(soon == 1, first, jnp.where(later == 1, second, third))
            first, second, third = first + soon, second + later - soon, third - (1 - later)
            for n in range(LINES):
                order[n // 4] = order[n // 4] + jnp.where(at == n, r * 16 ** (n % 4), 0)
        return [lax.rem(lax.div(order[n // 4], 16 ** (n % 4)), 16) for n in range(LINES)]

    barrier = pltpu.get_barrier_semaphore()
    for peer in (
        (row_at(1, 0), col), (row_at(-1, 0), col), (row_at(0, 1), col), (row_at(0, -1), col),
        (row, col_at(1)), (row, col_at(-1)), (row, col_at(0, False)),
    ):
        pl.semaphore_signal(barrier, inc=1, device_id=peer, device_id_type=MESH)

    body = pl.ds(HEAD, ROWS)
    fetch = [
        pltpu.make_async_copy(tiles, right.at[0, row, body], tsem.at[0]),
        pltpu.make_async_copy(tiles, left.at[0, col, body], tsem.at[1]),
    ]
    for copy in fetch:
        copy.start()
    n_row = lax.broadcasted_iota(jnp.int32, (HEAD, BS), 0)
    head = jnp.zeros((HEAD, BS), jnp.float32)
    for n in range(BLOCKS):
        entry = jnp.broadcast_to(pattern[n % 2 : n % 2 + 1, n // 2 : n // 2 + 1], (HEAD, BS)).astype(jnp.float32)
        head = jnp.where(n_row == n, entry, head)
    right[0, row, 0:HEAD] = head.astype(jnp.bfloat16)
    left[0, col, 0:HEAD] = head.astype(jnp.bfloat16)
    for copy in fetch:
        copy.wait()
    pl.semaphore_wait(barrier, 7)

    @pl.loop(0, ITERS)
    def _(it):
        g, m = (it, 0), (it, 1)

        row_start(g)
        col_start(it)
        acc[...] = jnp.zeros_like(acc)
        order = order_pieces()

        @pl.when(it == 0)
        def _():
            codes[...] = jnp.zeros_like(codes)
            for k in range(GROUP):
                loc[k, BLOCKS] = jnp.zeros((BS, BS), jnp.bfloat16)
            right[1, row, 0:HEAD] = right[0, row, 0:HEAD]
            left[1, col, 0:HEAD] = left[0, col, 0:HEAD]

        col_event(it, 0,1)
        row_e1(g)
        col_event(it, 2,3)
        row_fan(g, 0)
        row_e3(g)
        col_event(it, 4,5,6)
        row_fan(g, -1)
        col_event(it, 7,8)
        row_fan(g, 1)
        col_event(it, 9,10,11)
        row_fan(g, 2)
        row_last(g, 0)
        cross_wait(it, 0,1,2)

        @pl.when(it == 0)
        def _():
            make_table(
                [row_at(dx, dy) for dx in (-1, 0, 1, 2) for dy in (-1, 0, 1, 2) if abs(dx) + abs(dy) <= 2],
                [col_at(dz) for dz in range(-3, 4)] + [col_at(dz, False) for dz in range(-2, 3)],
            )

        col_event(it, 12)
        pieces(it, 0, order[:7])
        row_last(g, -1)
        col_event(it, 13)
        row_last(g, 1)

        @pl.when(it == 0)
        def _():
            make_table([row_at(2, -1), row_at(2, 1), row_at(-1, 2), row_at(1, 2)], [col_at(4)])

        pieces(it, 0, order[7:12])
        row_last(g, 2)
        cross_wait(it, 3, 4, 5)

        @pl.when(it == 0)
        def _():
            make_table([row_at(2, 2)], [col_at(dz, False) for dz in (-3, 3, 4)])

        pieces(it, 0, order[12:])

        scale = 1.0 / (2.0 * 2 * LINES * BS)
        def square_half(h):
            for i in (2 * h, 2 * h + 1):
                for t in range(2):
                    new = (acc[i, :, t * BS : (t + 1) * BS] * scale).astype(jnp.bfloat16)
                    mid[it, row, pl.ds((2 * i + t) * BS, BS)] = new
                    square_out[i, t] = new

        row_start(m, square_half)
        acc[...] = jnp.zeros_like(acc)
        row_e1(m)
        row_e3(m)
        row_fan(m, 0)
        row_fan(m, -1)
        pieces(it, 1, [row_at(0, 0), row_at(-1, 0), row_at(1, 0)])
        row_fan(m, 1)
        pieces(it, 1, [row_at(0, -1), row_at(0, 1)])
        row_fan(m, 2)
        pieces(it, 1, [row_at(-1, -1), row_at(-1, 1), row_at(1, -1), row_at(1, 1)])
        row_last(m, 0)
        pieces(it, 1, [row_at(2, 0), row_at(0, 2)])
        for f in (-1, 1):
            row_last(m, f)
            pieces(it, 1, [row_at(2, f), row_at(f, 2)])
        row_last(m, 2)
        pieces(it, 1, [row_at(2, 2)])

        def new_sign(i, t):
            s = left[it, col, block(2 * i + t)].astype(jnp.float32)
            new = 1.5 * s - 0.5 * acc[i, :, t * BS : (t + 1) * BS]
            return jnp.where(used[0, 4 * i + t] > 0, new, 0.0).astype(jnp.bfloat16)

        @pl.when(it < ITERS - 1)
        def _():
            for n in range(BLOCKS):
                now = new_sign(n // 2, n % 2)
                right[it + 1, row, block(n)] = now
                left[it + 1, col, block(n)] = now

        @pl.when(it == ITERS - 1)
        def _():
            for n in range(BLOCKS):
                sign_out[n // 2, n % 2] = new_sign(n // 2, n % 2)

    for it in range(ITERS):
        sent(right, rsend.at[it, 0])
        sent(mid, rsend.at[it, 1])
        sent(left, csend.at[it])


def shards(tiles, pattern):
    shape = jax.ShapeDtypeStruct(tiles.shape, tiles.dtype)
    vmem = pl.BlockSpec(memory_space=pltpu.VMEM)
    dma = pltpu.SemaphoreType.DMA
    both = pl.pallas_call(
        kernel,
        out_shape=jax.ShapeDtypeStruct((2,) + tiles.shape, tiles.dtype),
        in_specs=[pl.BlockSpec(memory_space=pltpu.HBM), vmem],
        out_specs=vmem,
        scratch_shapes=[
            pltpu.VMEM((ITERS, LINES, HEAD + ROWS, BS), jnp.bfloat16),
            pltpu.VMEM((ITERS, LINES, HEAD + ROWS, BS), jnp.bfloat16),
            pltpu.VMEM((ITERS, LINES, ROWS, BS), jnp.bfloat16),
            pltpu.VMEM((GROUP, BLOCKS + 1, BS, BS), jnp.bfloat16),
            pltpu.VMEM((4, BS, 2 * BS), jnp.float32),
            pltpu.VMEM((2, LINES, BS), jnp.float32),
            pltpu.VMEM((2, LINES, BS), jnp.int32),
            pltpu.SMEM((LINES, BS), jnp.int32),
            pltpu.SMEM((LINES, BS), jnp.int32),
            dma((2,)),
            dma((2,)),
            dma((ITERS, 2)),
            dma((ITERS, 2, len(ROW_KEYS))),
            dma((ITERS,)),
            dma((ITERS, len(COL_ID))),
        ],
        compiler_params=pltpu.CompilerParams(
            collective_id=0, has_side_effects=True, vmem_limit_bytes=48 * 1024 * 1024
        ),
    )(tiles.reshape(ROWS, BS), pattern.T)
    return both[0], both[1]


def solution(mesh):
    return jax.shard_map(
        shards,
        mesh=mesh,
        in_specs=(P("row", "col", None, None), P("row", "col")),
        out_specs=(P("row", "col", None, None), P("row", "col", None, None)),
        check_vma=False,
    )
```

```python
import jax
import jax.numpy as jnp
from jax import lax
from jax.experimental import pallas as pl
from jax.experimental.pallas import tpu as pltpu
from jax.sharding import PartitionSpec as P

ITERS = 2
SIDE = 4
RING = 8
LINES = 16
BLOCKS = 8
BS = 128
GROUP = 7
HEAD = 16
ROWS = BLOCKS * BS
MESH = pl.DeviceIdType.MESH

PARTS = {"w": (0, 4), "a": (0, 2), "b": (2, 4)}
ROW_KEYS = []
for _h in (0, 1):
    ROW_KEYS += [(_h, -1, 0, "w"), (_h, 1, 0, "w"), (_h, 2, 0, "a"), (_h, 2, 0, "b")]
    for _f in (0, -1, 1, 2):
        ROW_KEYS += [(_h, _f, -1, "w"), (_h, _f, 1, "w"), (_h, _f, 2, "a"), (_h, _f, 2, "b")]
ROW_ID = {key: n for n, key in enumerate(ROW_KEYS)}

UP = [(1, q, d) for d in (1, 2, 3) for q in (0, 1, 2, 3)] + [(1, q, 4) for q in (0, 1)]
DOWN = [(-1, q, d) for d in (1, 2, 3) for q in (2, 3, 0, 1)] + [(-1, q, 4) for q in (2, 3)]
CROSS = [("c", 1, 0)] + [("c", s, d) for d in (1, 2, 3, 4, 5) for s in (1, -1)]
COL_ID = {key: n for n, key in enumerate(UP + DOWN + CROSS)}


def kernel(
    tiles, pattern, out,
    left, right, mid, loc, acc, codes, pv, table, used,
    tsem, psem, rsend, rrecv, csend, crecv,
):
    sign_out, square_out = out.at[0], out.at[1]
    row, col = lax.axis_index("row"), lax.axis_index("col")
    x, y = lax.div(row, SIDE), lax.rem(row, SIDE)
    z, core = lax.div(col, 2), lax.rem(col, 2)

    def row_at(dx, dy):
        return lax.rem(x + dx + SIDE, SIDE) * SIDE + lax.rem(y + dy + SIDE, SIDE)

    def col_at(dz, own_core=True):
        return lax.rem(z + dz + RING, RING) * 2 + (core if own_core else 1 - core)

    def block(n):
        return pl.ds(HEAD + n * BS, BS)

    def row_copy(it, which, key, sending):
        h, f, s, part = key
        second = s != 0
        step = {-1: 1, 1: -1}.get(s if second else f) or (1 if part == "a" else -1)
        if sending:
            if second:
                s = s + step if s != 2 else -step
            else:
                f = f + step if f != 2 else -step
        lo, hi = ((h * 4 + p) * BS for p in PARTS[part])
        off = (f, s) if h == 0 else (s, f)
        if which == 0:
            lo, hi = lo + HEAD if lo else 0, hi + HEAD
        ref = (right, mid)[which].at[it, row_at(*off), pl.ds(lo, hi - lo)]
        target = row_at(step, 0) if (h == 0) != second else row_at(0, step)
        return pltpu.make_async_remote_copy(
            src_ref=ref, dst_ref=ref, send_sem=rsend.at[it, which], recv_sem=rrecv.at[it, which, ROW_ID[key]],
            device_id=(target, col), device_id_type=MESH,
        )

    def row_send(g, *keys):
        for key in keys:
            row_copy(*g, key, True).start()

    def row_wait(g, *keys):
        for key in keys:
            row_copy(*g, key, False).wait_recv()

    def col_copy(it, key, sending):
        sign, d = key[-3] if key[0] != "c" else key[1], key[-1]
        if key[0] == "c":
            ref_col = col_at(-sign * min(d, 4), sending)
            target = col_at(0, False)
            lo = d - 4 if sign == 1 else d - 2
            lo, hi = (0, 4) if d < 4 else (lo, lo + 1)
        else:
            ref_col = col_at(-sign * (d - 1 if sending else d))
            target = col_at(sign)
            lo, hi = key[1], key[1] + 1
        lo, hi = lo * 2 * BS + HEAD if lo else 0, hi * 2 * BS + HEAD
        ref = left.at[it, ref_col, pl.ds(lo, hi - lo)]
        return pltpu.make_async_remote_copy(
            src_ref=ref, dst_ref=ref, send_sem=csend.at[it], recv_sem=crecv.at[it, COL_ID[key]],
            device_id=(row, target), device_id_type=MESH,
        )

    def col_start(it):
        for up, down in zip(UP[:4], DOWN[:4]):
            col_copy(it, up, True).start()
            col_copy(it, down, True).start()
        col_copy(it, CROSS[0], True).start()

    def col_event(it, *ns):
        for n in ns:
            for key in (UP[n], DOWN[n]):
                col_copy(it, key, False).wait_recv()
                sign, q, d = key
                if (sign, q, d + 1) in COL_ID:
                    col_copy(it, (sign, q, d + 1), True).start()
                if n % 4 == 3 or n >= 12:
                    col_copy(it, ("c", sign, d + (n == 13)), True).start()

    def cross_wait(it, *ds):
        for key in CROSS:
            if key[2] in ds:
                col_copy(it, key, False).wait_recv()

    def row_start(g, ready=lambda h: None):
        for h in (0, 1):
            ready(h)
            row_send(g, (h, -1, 0, "w"), (h, 1, 0, "w"))
        for h in (1, 0):
            row_send(g, (h, 0, -1, "w"), (h, 0, 1, "w"))

    def row_e1(g):
        for h in (0, 1):
            for f, part in ((-1, "a"), (1, "b")):
                row_wait(g, (h, f, 0, "w"))
                row_send(g, (h, 2, 0, part))
        for f in (-1, 1):
            for h in (0, 1):
                row_send(g, (h, f, -1, "w"), (h, f, 1, "w"))

    def row_e3(g):
        for h in (0, 1):
            row_wait(g, (h, 2, 0, "a"), (h, 2, 0, "b"))
            row_send(g, (h, 2, -1, "w"), (h, 2, 1, "w"))

    def row_fan(g, f):
        for h in (1, 0):
            for s, part in ((-1, "a"), (1, "b")):
                row_wait(g, (h, f, s, "w"))
                row_send(g, (h, f, 2, part))

    def row_last(g, *fs):
        for f in fs:
            for h in (0, 1):
                row_wait(g, (h, f, 2, "a"), (h, f, 2, "b"))

    def sent(ref, sem):
        some = ref.at[0, pl.ds(0, LINES - 1)]
        pltpu.make_async_copy(some, some, sem).wait()

    def pieces(it, which, rs):
        head = HEAD if which == 0 else 0
        for g, r in enumerate(rs):
            for n in range(BLOCKS):
                loc[g, n] = (right, mid)[which][it, r, pl.ds(head + n * BS, BS)]
            for i in range(4):
                a = jnp.concatenate([left[it, r, block(2 * i)], left[it, r, block(2 * i + 1)]], axis=1)
                b = [[loc[g, table[r, 4 * i + 2 * s + t]] for t in (0, 1)] for s in (0, 1)]
                b = jnp.concatenate([jnp.concatenate(pair, axis=1) for pair in b], axis=0)
                acc[i] += jnp.dot(a, b, preferred_element_type=jnp.float32)

    def apart(a, b, n):
        d = lax.rem(a - b + n, n)
        return jnp.minimum(d, n - d)

    def decode(tile):
        at = lax.broadcasted_iota(jnp.int32, (HEAD, BS), 0)
        weight = jnp.where(at < BLOCKS, 1 << (3 * jnp.minimum(at, BLOCKS - 1)), 0).astype(jnp.float32)
        return jnp.sum(tile.astype(jnp.float32) * weight, axis=0, keepdims=True)

    def make_table(rows, cols):
        for r in rows:
            codes[0, pl.ds(r, 1)] = decode(right[0, r, 0:HEAD])
        for c in cols:
            codes[1, pl.ds(c, 1)] = decode(left[0, c, 0:HEAD])
        ones = sum(1 << (3 * n) for n in range(BLOCKS))
        theirs, mine = codes[0].astype(jnp.int32) + ones, codes[1].astype(jnp.int32) + ones
        own = jnp.broadcast_to(decode(left[0, col, 0:HEAD]), (LINES, BS)).astype(jnp.int32) + ones
        lane = lax.broadcasted_iota(jnp.int32, (LINES, BS), 1) & 15
        i, s, t = lane >> 2, (lane >> 1) & 1, lane & 1
        k = ((mine >> (6 * i + 3 * s)) & 7) - 1
        at_k = jnp.clip(k, 0, SIDE - 1)
        pair = theirs >> (6 * at_k)
        j = (own >> (6 * i + 3 * t)) & 7
        found = jnp.where((pair & 7) == j, 2 * at_k, jnp.where(((pair >> 3) & 7) == j, 2 * at_k + 1, BLOCKS))
        pv[0] = jnp.where((k >= 0) & (j > 0), found, BLOCKS)
        pv[1] = j
        copies = [pltpu.make_async_copy(pv.at[n], (table, used)[n], psem.at[n]) for n in (0, 1)]
        for copy in copies:
            copy.start()
        for copy in copies:
            copy.wait()

    def order_pieces():
        ranks = []
        for r in range(LINES):
            dx, dy, dz = apart(r // SIDE, x, SIDE), apart(r % SIDE, y, SIDE), apart(r // 2, z, RING)
            mine = core == r % 2
            soon = (dx + dy <= 2) & ((dz <= 2) | (mine & (dz <= 3)))
            later = (dx + dy <= 3) & ((dz <= 2) | mine)
            ranks.append((soon.astype(jnp.int32), later.astype(jnp.int32)))
        first, second, third = jnp.int32(0), sum(soon for soon, _ in ranks), jnp.int32(LINES - 1)
        order = [jnp.int32(0)] * 4
        for r, (soon, later) in enumerate(ranks):
            at = jnp.where(soon == 1, first, jnp.where(later == 1, second, third))
            first, second, third = first + soon, second + later - soon, third - (1 - later)
            for n in range(LINES):
                order[n // 4] = order[n // 4] + jnp.where(at == n, r * 16 ** (n % 4), 0)
        return [lax.rem(lax.div(order[n // 4], 16 ** (n % 4)), 16) for n in range(LINES)]

    barrier = pltpu.get_barrier_semaphore()
    for peer in (
        (row_at(1, 0), col), (row_at(-1, 0), col), (row_at(0, 1), col), (row_at(0, -1), col),
        (row, col_at(1)), (row, col_at(-1)), (row, col_at(0, False)),
    ):
        pl.semaphore_signal(barrier, inc=1, device_id=peer, device_id_type=MESH)

    body = pl.ds(HEAD, ROWS)
    fetch = [
        pltpu.make_async_copy(tiles, right.at[0, row, body], tsem.at[0]),
        pltpu.make_async_copy(tiles, left.at[0, col, body], tsem.at[1]),
    ]
    for copy in fetch:
        copy.start()
    n_row = lax.broadcasted_iota(jnp.int32, (HEAD, BS), 0)
    head = jnp.zeros((HEAD, BS), jnp.float32)
    for n in range(BLOCKS):
        entry = jnp.broadcast_to(pattern[n % 2 : n % 2 + 1, n // 2 : n // 2 + 1], (HEAD, BS)).astype(jnp.float32)
        head = jnp.where(n_row == n, entry, head)
    right[0, row, 0:HEAD] = head.astype(jnp.bfloat16)
    left[0, col, 0:HEAD] = head.astype(jnp.bfloat16)
    for copy in fetch:
        copy.wait()
    pl.semaphore_wait(barrier, 7)

    @pl.loop(0, ITERS)
    def _(it):
        g, m = (it, 0), (it, 1)

        @pl.when(it == 0)
        def _():
            row_start(g)

        col_start(it)
        acc[...] = jnp.zeros_like(acc)
        order = order_pieces()

        @pl.when(it == 0)
        def _():
            codes[...] = jnp.zeros_like(codes)
            for k in range(GROUP):
                loc[k, BLOCKS] = jnp.zeros((BS, BS), jnp.bfloat16)
            right[1, row, 0:HEAD] = right[0, row, 0:HEAD]
            left[1, col, 0:HEAD] = left[0, col, 0:HEAD]

        col_event(it, 0,1)
        row_e1(g)
        col_event(it, 2,3)
        row_fan(g, 0)
        row_e3(g)
        col_event(it, 4,5,6)
        row_fan(g, -1)
        col_event(it, 7,8)
        row_fan(g, 1)
        col_event(it, 9,10,11)
        row_fan(g, 2)
        row_last(g, 0)
        cross_wait(it, 0,1,2)

        @pl.when(it == 0)
        def _():
            make_table(
                [row_at(dx, dy) for dx in (-1, 0, 1, 2) for dy in (-1, 0, 1, 2) if abs(dx) + abs(dy) <= 2],
                [col_at(dz) for dz in range(-3, 4)] + [col_at(dz, False) for dz in range(-2, 3)],
            )

        col_event(it, 12)
        pieces(it, 0, order[:7])
        row_last(g, -1)
        col_event(it, 13)
        row_last(g, 1)

        @pl.when(it == 0)
        def _():
            make_table([row_at(2, -1), row_at(2, 1), row_at(-1, 2), row_at(1, 2)], [col_at(4)])

        pieces(it, 0, order[7:12])
        row_last(g, 2)
        cross_wait(it, 3, 4, 5)

        @pl.when(it == 0)
        def _():
            make_table([row_at(2, 2)], [col_at(dz, False) for dz in (-3, 3, 4)])

        pieces(it, 0, order[12:])

        scale = 1.0 / (2.0 * 2 * LINES * BS)
        def square_half(h):
            for i in (2 * h, 2 * h + 1):
                for t in range(2):
                    new = (acc[i, :, t * BS : (t + 1) * BS] * scale).astype(jnp.bfloat16)
                    mid[it, row, pl.ds((2 * i + t) * BS, BS)] = new
                    square_out[i, t] = new

        row_start(m, square_half)
        acc[...] = jnp.zeros_like(acc)
        row_e1(m)
        row_e3(m)
        row_fan(m, 0)
        row_fan(m, -1)
        pieces(it, 1, [row_at(0, 0), row_at(-1, 0), row_at(1, 0)])
        row_fan(m, 1)
        pieces(it, 1, [row_at(0, -1), row_at(0, 1)])
        row_fan(m, 2)
        pieces(it, 1, [row_at(-1, -1), row_at(-1, 1), row_at(1, -1), row_at(1, 1)])
        row_last(m, 0)
        pieces(it, 1, [row_at(2, 0), row_at(0, 2)])
        for f in (-1, 1):
            row_last(m, f)
            pieces(it, 1, [row_at(2, f), row_at(f, 2)])
        row_last(m, 2)
        pieces(it, 1, [row_at(2, 2)])

        def new_sign(i, t):
            s = left[it, col, block(2 * i + t)].astype(jnp.float32)
            new = 1.5 * s - 0.5 * acc[i, :, t * BS : (t + 1) * BS]
            return jnp.where(used[0, 4 * i + t] > 0, new, 0.0).astype(jnp.bfloat16)

        @pl.when(it < ITERS - 1)
        def _():
            def sign_half(h):
                for n in range(4 * h, 4 * h + 4):
                    now = new_sign(n // 2, n % 2)
                    right[it + 1, row, block(n)] = now
                    left[it + 1, col, block(n)] = now

            row_start((it + 1, 0), sign_half)

        @pl.when(it == ITERS - 1)
        def _():
            for n in range(BLOCKS):
                sign_out[n // 2, n % 2] = new_sign(n // 2, n % 2)

    for it in range(ITERS):
        sent(right, rsend.at[it, 0])
        sent(mid, rsend.at[it, 1])
        sent(left, csend.at[it])


def shards(tiles, pattern):
    shape = jax.ShapeDtypeStruct(tiles.shape, tiles.dtype)
    vmem = pl.BlockSpec(memory_space=pltpu.VMEM)
    dma = pltpu.SemaphoreType.DMA
    both = pl.pallas_call(
        kernel,
        out_shape=jax.ShapeDtypeStruct((2,) + tiles.shape, tiles.dtype),
        in_specs=[pl.BlockSpec(memory_space=pltpu.HBM), vmem],
        out_specs=vmem,
        scratch_shapes=[
            pltpu.VMEM((ITERS, LINES, HEAD + ROWS, BS), jnp.bfloat16),
            pltpu.VMEM((ITERS, LINES, HEAD + ROWS, BS), jnp.bfloat16),
            pltpu.VMEM((ITERS, LINES, ROWS, BS), jnp.bfloat16),
            pltpu.VMEM((GROUP, BLOCKS + 1, BS, BS), jnp.bfloat16),
            pltpu.VMEM((4, BS, 2 * BS), jnp.float32),
            pltpu.VMEM((2, LINES, BS), jnp.float32),
            pltpu.VMEM((2, LINES, BS), jnp.int32),
            pltpu.SMEM((LINES, BS), jnp.int32),
            pltpu.SMEM((LINES, BS), jnp.int32),
            dma((2,)),
            dma((2,)),
            dma((ITERS, 2)),
            dma((ITERS, 2, len(ROW_KEYS))),
            dma((ITERS,)),
            dma((ITERS, len(COL_ID))),
        ],
        compiler_params=pltpu.CompilerParams(
            collective_id=0, has_side_effects=True, vmem_limit_bytes=48 * 1024 * 1024
        ),
    )(tiles.reshape(ROWS, BS), pattern.T)
    return both[0], both[1]


def solution(mesh):
    return jax.shard_map(
        shards,
        mesh=mesh,
        in_specs=(P("row", "col", None, None), P("row", "col")),
        out_specs=(P("row", "col", None, None), P("row", "col", None, None)),
        check_vma=False,
    )
```
